128 devices in a mesh: ctx: 8 (over z, x_lo), fsdp: 16 (over y, x_hi, core).
Axes of the slice: x: 4 (x_hi: 2, x_lo: 2; x = x_hi * 2 + x_lo), y: 4, z: 4, core: 2. Of those that a mesh axis runs over, the one named last changes fastest.
Arguments:
- inputs: bfloat16 [16, 1024, 1024], P('fsdp', 'ctx'), may hold values from -6 to 6
- segments: int32 [16, 1024], P('fsdp', 'ctx'), may hold values from 0 to 3, as said below
- routes: int32 [16, 1024, 8], P('fsdp', 'ctx'), may hold values from 0 to 31, all different within a row; in each aligned block of 128 rows (0 to 127, 128 to 255, ..., all dimensions but the last counted through in order) at most 40 rows name the same one
- gate_weights: float32 [16, 1024, 8], P('fsdp', 'ctx'), may hold values from 0.06 to 0.19
- cotangent: bfloat16 [16, 1024, 1024], P('fsdp', 'ctx'), may hold values from -6 to 6
- norm_in: bfloat16 [1024], P('fsdp'), may hold values from 0.5 to 1.5
- norm_mid: bfloat16 [1024], P('fsdp'), may hold values from 0.5 to 1.5
- q_gain: bfloat16 [64], replicated, may hold values from 0.5 to 1.5
- k_gain: bfloat16 [64], replicated, may hold values from 0.5 to 1.5
- w_query: bfloat16 [1024, 1024], P('fsdp'), may hold values from -0.1875 to 0.1875
- w_key: bfloat16 [1024, 512], P('fsdp'), may hold values from -0.1875 to 0.1875
- w_value: bfloat16 [1024, 512], P('fsdp'), may hold values from -0.1875 to 0.1875
- w_out: bfloat16 [1024, 1024], P('fsdp'), may hold values from -4 to 4
- w_gate: bfloat16 [32, 1024, 512], P('fsdp'), may hold values from -0.1875 to 0.1875
- w_up: bfloat16 [32, 1024, 512], P('fsdp'), may hold values from -0.1875 to 0.1875
- w_down: bfloat16 [32, 512, 1024], P('fsdp'), may hold values from -1.25 to 1.25
Outputs:
- output: bfloat16 [16, 1024, 1024], P('fsdp', 'ctx')
- input_grad: float32 [16, 1024, 1024], P('fsdp', 'ctx')
- grad_norm_in: float32 [1024], P('fsdp')
- grad_norm_mid: float32 [1024], P('fsdp')
- grad_q_gain: float32 [64], replicated
- grad_k_gain: float32 [64], replicated
- grad_query: float32 [1024, 1024], P('fsdp')
- grad_key: float32 [1024, 512], P('fsdp')
- grad_value: float32 [1024, 512], P('fsdp')
- grad_out: float32 [1024, 1024], P('fsdp')
- grad_gate: float32 [32, 1024, 512], P('fsdp')
- grad_up: float32 [32, 1024, 512], P('fsdp')
- grad_down: float32 [32, 512, 1024], P('fsdp')
The draws below stay inside these ranges and needn't reach their ends.
Inputs may be any that keep to these rules, and one draw needn't show every extreme that they name: `segments`: read in the order of pos, the document numbers of a sequence never fall. `routes`: each token names 8 different experts. In every group of 128 consecutive stored rows of a sequence no expert is named by more than 40 tokens.
All inputs are finite; a program needn't handle non-finite values.
Results may differ from the reference program's by a relative error of at most 0.025.
Values may be sent and summed in bfloat16 or wider, within the bound.
A program may use at most 128 MiB of HBM per device.

```python
import math
from functools import partial
import jax
import jax.numpy as jnp
import numpy as np
from jax import lax

D = 1024
H = 16
KVH = 8
DH = 64
FF = 512
EXPERTS = 32
TOP = 8
BLK = 64
DOCS = 4
CAP = 40
LEN = 1024
SEQS = 16


def draw_segments(key, part):
    key = jax.random.fold_in(key, 11)
    first_key, later_key, side_key = jax.random.split(key, 3)
    first_cut = jax.random.randint(first_key, (SEQS, 1), LEN // 2, 3 * LEN // 4 + 1)
    later_cuts = jax.random.randint(later_key, (SEQS, DOCS - 2), first_cut + 1, LEN)
    cuts = jnp.concatenate([first_cut, later_cuts], axis=1)
    flipped = jax.random.randint(side_key, (SEQS, 1), 0, 2)
    natural_pos = jnp.arange(LEN, dtype=jnp.int32)[None, :]
    probe = jnp.where(flipped == 1, LEN - 1 - natural_pos, natural_pos)
    counted = jnp.sum((probe[:, :, None] >= cuts[:, None, :]).astype(jnp.int32), axis=-1)
    natural_seg = jnp.where(flipped == 1, DOCS - 1 - counted, counted)
    n_blocks = LEN // BLK
    indices = jnp.arange(LEN, dtype=jnp.int32)
    stored_block = indices // BLK
    natural = jnp.where(stored_block % 2 == 0, stored_block // 2, n_blocks - 1 - stored_block // 2)
    stored = natural * BLK + indices % BLK
    return jnp.take_along_axis(natural_seg, jnp.broadcast_to(stored[None, :], (SEQS, LEN)), axis=1).astype(jnp.int32)


def level_of(rng, extent, cuts, least, high):
    level = 1.0
    for dim, parts in cuts:
        heights = jax.random.uniform(jax.random.fold_in(jax.random.fold_in(rng, 6), dim), (parts,), jnp.float32, least / len(cuts), high / len(cuts))
        level = level * jnp.repeat(jnp.exp(heights), extent[dim] // parts).reshape((-1,) + (1,) * (len(extent) - 1 - dim))
    return level


def routed_block(own_key, own, number, rows, number_of, top, most, lean):
    order = jax.random.permutation(own_key, number_of)
    crowded, ordinary = shares(number_of, rows * top, most, lean, True), shares(number_of, rows * top, most, lean, False)
    places = jnp.arange(number_of)

    def named(tallies, rotation):
        used = int((tallies > 0).sum())
        fixed = max(1, used // 4)
        shifted = fixed + (places - fixed + rotation * (used - fixed)) % max(1, number_of - fixed)
        return jnp.zeros((number_of,), jnp.int32).at[order[jnp.where(places < fixed, places, shifted)]].set(jnp.asarray(tallies, jnp.int32))

    tallies = jnp.where(number % 4 == 0, named(crowded, number // 4), named(ordinary, number - number // 4 - 1))
    mixed = jax.random.permutation(jax.random.fold_in(own, 3), number_of)
    giver, receiver = mixed[0:number_of // 2 * 2:2], mixed[1:number_of // 2 * 2:2]
    margin = jnp.minimum(tallies[giver] - 1, most - tallies[receiver]) // 2
    margin = jnp.where((giver == order[0]) | (receiver == order[0]) | (tallies[receiver] == 0), 0, jnp.maximum(margin, 0))
    shifted = jax.random.randint(jax.random.fold_in(own, 4), (number_of // 2,), 0, 1 << 20) % (margin + 1)
    tallies = tallies.at[giver].add(-shifted).at[receiver].add(shifted)
    members = jnp.searchsorted(jnp.cumsum(tallies), jnp.arange(rows * top), side="right").astype(jnp.int32)
    table = members.reshape(top, rows).T
    table = table[jax.random.permutation(jax.random.fold_in(own, 1), rows)]
    rotation = jax.random.randint(jax.random.fold_in(own, 2), (rows, 1), 0, top)
    return jnp.take_along_axis(table, (jnp.arange(top)[None, :] + rotation) % top, axis=1)


def shares(amount, total, most, skew, full):
    loads = [(1 << 20) // math.isqrt(standing ** skew) + 1 for standing in range(1, amount + 1)]
    largest = most if full else min(most, max(-(-total // amount), total * loads[0] // sum(loads)))
    least = 1 if total - largest >= amount - 1 else 0
    holding, spare = [largest] + [least] * (amount - 1), total - largest - least * (amount - 1)
    while spare > 0:
        candidates = [i for i in range(1, amount) if holding[i] < largest] or [i for i in range(1, amount) if holding[i] < most]
        whole, budget = sum([loads[i] for i in candidates]), spare
        for i in candidates:
            addition = min(most - holding[i], max(1, budget * loads[i] // whole), spare)
            holding[i] = holding[i] + addition
            spare = spare - addition
    return np.array(holding)


def bell_draw(rng, shape, width, limit, pieces=(), held_as=jnp.bfloat16):
    loudness = level_of(rng, shape, pieces, -0.22, 0.18) if pieces else 1.0
    values = jax.random.normal(rng, shape, jnp.float32) * width * loudness
    return jnp.minimum(jnp.maximum(values, -limit), limit).astype(held_as)


def setup_inputs(seed: int = 0) -> dict:
    seeds = jax.random.split(jax.random.key(seed), 17)
    inputs = bell_draw(seeds[0], (SEQS, LEN, D), 1.0, 6.0, ((0, 16), (1, 8)))
    segments = draw_segments(jax.random.fold_in(seeds[16], 71), 0)
    routes_keys = jax.random.split(jax.random.fold_in(seeds[2], 1), SEQS * LEN // (2 * BLK))
    routes_turns = jax.random.permutation(jax.random.fold_in(seeds[2], 3), SEQS * LEN // (2 * BLK))
    routes = jax.vmap(lambda own, number: routed_block(jax.random.fold_in(seeds[2], 2), own, number, 2 * BLK, EXPERTS, TOP, CAP, 1))(routes_keys, routes_turns).reshape((SEQS, LEN, TOP))
    gate_weights = jnp.clip(0.06 + 0.13 * jax.random.uniform(seeds[3], (SEQS, LEN, TOP), jnp.float32) ** level_of(seeds[3], (SEQS, LEN, TOP), ((0, 16), (1, 8)), -0.2, 0.2), 0.06, 0.19)
    cotangent = bell_draw(seeds[4], (SEQS, LEN, D), 1.0, 6.0, ((0, 16), (1, 8)))
    norm_in = jnp.clip(1.0 + 0.1 * jax.random.normal(seeds[5], (D,), jnp.float32), 0.5, 1.5).astype(jnp.bfloat16)
    norm_mid = jnp.clip(1.0 + 0.1 * jax.random.normal(seeds[6], (D,), jnp.float32), 0.5, 1.5).astype(jnp.bfloat16)
    q_gain = jnp.clip(1.0 + 0.1 * jax.random.normal(seeds[7], (DH,), jnp.float32), 0.5, 1.5).astype(jnp.bfloat16)
    k_gain = jnp.clip(1.0 + 0.1 * jax.random.normal(seeds[8], (DH,), jnp.float32), 0.5, 1.5).astype(jnp.bfloat16)
    w_query = bell_draw(seeds[9], (D, H * DH), D ** -0.5, 0.1875, ((0, 16),))
    w_key = bell_draw(seeds[10], (D, KVH * DH), D ** -0.5, 0.1875, ((0, 16),))
    w_value = bell_draw(seeds[11], (D, KVH * DH), D ** -0.5, 0.1875, ((0, 16),))
    w_out = bell_draw(seeds[12], (H * DH, D), (max(2 * H * DH // LEN, 1)) ** -0.5, 4.0, ((0, 16),))
    w_gate = bell_draw(seeds[13], (EXPERTS, D, FF), D ** -0.5, 0.1875, ((0, 16),))
    w_up = bell_draw(seeds[14], (EXPERTS, D, FF), D ** -0.5, 0.1875, ((0, 16),))
    w_down = bell_draw(seeds[15], (EXPERTS, FF, D), (max(FF // 25, 1)) ** -0.5, 1.25, ((0, 16),))
    return {"inputs": inputs, "segments": segments, "routes": routes, "gate_weights": gate_weights, "cotangent": cotangent, "norm_in": norm_in, "norm_mid": norm_mid, "q_gain": q_gain, "k_gain": k_gain, "w_query": w_query, "w_key": w_key, "w_value": w_value, "w_out": w_out, "w_gate": w_gate, "w_up": w_up, "w_down": w_down}


@jax.custom_vjp
def low(v):
    return lax.optimization_barrier(v.astype(jnp.bfloat16)).astype(jnp.float32)

@jax.custom_vjp
def low_back(v):
    return v

def low_keep(v):
    return (low(v), None)

def low_pass(kept, grad):
    return (grad,)

def back_keep(v):
    return (v, None)

def back_low(kept, grad):
    return (low(grad),)
low.defvjp(low_keep, low_pass)
low_back.defvjp(back_keep, back_low)
highest = lax.Precision.HIGHEST

def rms_scale(values, gain_vec, epsilon):
    return values * lax.rsqrt(lax.optimization_barrier(jnp.mean(values * values, axis=-1, keepdims=True)) + epsilon) * gain_vec

def rotary(values, positions):
    head_dim = values.shape[-1]
    half_dim = head_dim // 2
    frequency = 10000.0 ** (-jnp.arange(half_dim, dtype=jnp.float32) * 2.0 / head_dim)
    angles = positions.astype(jnp.float32)[:, None] * frequency[None, :]
    cosine = jnp.cos(angles)[:, None, :]
    sine_val = jnp.sin(angles)[:, None, :]
    front_half = values[..., :half_dim]
    back_half = values[..., half_dim:]
    return jnp.concatenate([front_half * cosine - back_half * sine_val, back_half * cosine + front_half * sine_val], axis=-1)

def stored_positions():
    n_blocks = LEN // BLK
    indices = jnp.arange(LEN, dtype=jnp.int32)
    stored_block = indices // BLK
    natural = jnp.where(stored_block % 2 == 0, stored_block // 2, n_blocks - 1 - stored_block // 2)
    return natural * BLK + indices % BLK

def slot_targets(route_rows):
    onehot = (route_rows[:, :, None] == jnp.arange(EXPERTS, dtype=jnp.int32)[None, None, :]).astype(jnp.int32)
    running = jnp.cumsum(onehot.reshape(-1, EXPERTS), axis=0).reshape(onehot.shape)
    slot_pos = lax.optimization_barrier(jnp.sum(running * onehot, axis=-1)) - 1
    return route_rows * CAP + slot_pos

def attend_rows(query_rows, seg_rows, keys_all, values_all, seg_keys):
    score_scale = 1.0 / math.sqrt(DH)
    scores = low_back(jnp.einsum('qhgd,khd->hgqk', query_rows, keys_all, precision=highest) * score_scale)
    same_doc = (seg_rows[:, None] == seg_keys[None, :])[None, None]
    scores = jnp.where(same_doc, scores, -1e+30)
    row_peak = lax.optimization_barrier(jnp.max(scores, axis=-1, keepdims=True))
    exp_scores = jnp.exp(scores - row_peak)
    softmax_p = low(exp_scores / lax.optimization_barrier(jnp.sum(exp_scores, axis=-1, keepdims=True)))
    return jnp.einsum('hgqk,khd->qhgd', softmax_p, values_all, precision=highest)

def expert_block(normed_rows, route_rows, gate_rows, w_gate, w_up, w_down):
    targets = slot_targets(route_rows)
    slot_ids = jnp.arange(EXPERTS * CAP, dtype=jnp.int32)
    dispatch = lax.optimization_barrier(jnp.sum((targets[None, :, :] == slot_ids[:, None, None]).astype(jnp.float32), axis=-1))
    slots_in = low_back(jnp.dot(dispatch, normed_rows, precision=highest)).reshape(EXPERTS, CAP, D)
    gate_pre = low_back(jnp.einsum('ecd,edf->ecf', slots_in, w_gate, precision=highest))
    up_pre = low_back(jnp.einsum('ecd,edf->ecf', slots_in, w_up, precision=highest))
    act_low = low(jax.nn.silu(gate_pre) * up_pre)
    slots_out = low(low_back(jnp.einsum('ecf,efd->ecd', act_low, w_down, precision=highest))).reshape(EXPERTS * CAP, D)
    picked = slots_out[targets]
    return lax.optimization_barrier(jnp.sum(gate_rows[:, :, None] * picked, axis=1))

def layer(seq_rows, seg_ids, route_ids, gate_vals, positions, norm_in, norm_mid, q_gain, k_gain, w_query, w_key, w_value, w_out, w_gate, w_up, w_down):
    normed = low(rms_scale(seq_rows, norm_in, 1e-05))
    query_raw = low_back(jnp.dot(normed, w_query, precision=highest))
    key_raw = low_back(jnp.dot(normed, w_key, precision=highest))
    value_low = low(low_back(jnp.dot(normed, w_value, precision=highest)))
    query_rot = low(low_back(rotary(rms_scale(query_raw.reshape(LEN, H, DH), q_gain, 1e-06), positions)))
    key_rot = low(low_back(rotary(rms_scale(key_raw.reshape(LEN, KVH, DH), k_gain, 1e-06), positions)))
    rows_per = math.gcd(LEN, 512)
    query_blocks = query_rot.reshape(LEN // rows_per, rows_per, KVH, H // KVH, DH)
    seg_blocks = seg_ids.reshape(LEN // rows_per, rows_per)
    attend = jax.checkpoint(partial(attend_rows, keys_all=key_rot, values_all=value_low.reshape(LEN, KVH, DH), seg_keys=seg_ids))
    context = lax.map(lambda block_items: attend(block_items[0], block_items[1]), (query_blocks, seg_blocks))
    context = low(low_back(context.reshape(LEN, H * DH)))
    branch = low_back(jnp.dot(context, w_out, precision=highest))
    middle = seq_rows + branch
    normed_mid = low(rms_scale(middle, norm_mid, 1e-05))
    groups = LEN // (2 * BLK)
    expert_fn = partial(expert_block, w_gate=w_gate, w_up=w_up, w_down=w_down)
    expert_sum = jax.vmap(expert_fn)(normed_mid.reshape(groups, 2 * BLK, D), route_ids.reshape(groups, 2 * BLK, TOP), gate_vals.reshape(groups, 2 * BLK, TOP))
    return middle + expert_sum.reshape(LEN, D)

def reference(inputs, segments, routes, gate_weights, cotangent, norm_in, norm_mid, q_gain, k_gain, w_query, w_key, w_value, w_out, w_gate, w_up, w_down):
    params = tuple((weight.astype(jnp.float32) for weight in (norm_in, norm_mid, q_gain, k_gain, w_query, w_key, w_value, w_out, w_gate, w_up, w_down)))
    positions = stored_positions()

    def one_sequence(totals, seq_items):
        seq_rows, seg_ids, route_ids, gate_vals, seq_cot = seq_items

        def forward(rows_float, *weights):
            return layer(rows_float, seg_ids, route_ids, gate_vals.astype(jnp.float32), positions, *weights)
        result, pullback = jax.vjp(forward, seq_rows.astype(jnp.float32), *params)
        all_grads = pullback(seq_cot.astype(jnp.float32))
        new_totals = tuple((total_grad + one_grad for total_grad, one_grad in zip(totals, all_grads[1:])))
        return (new_totals, (result.astype(jnp.bfloat16), all_grads[0]))
    zero_grads = tuple((jnp.zeros(weight.shape, jnp.float32) for weight in params))
    totals, (outputs, input_grads) = lax.scan(one_sequence, zero_grads, (inputs, segments, routes, gate_weights, cotangent))
    return (outputs, input_grads, totals[0], totals[1], totals[2], totals[3], totals[4], totals[5], totals[6], totals[7], totals[8], totals[9], totals[10])
```

```python
import math

import jax
import jax.numpy as jnp
import numpy as np
from jax import lax
from jax.experimental import pallas as pl
from jax.experimental.pallas import tpu as pltpu
from jax.sharding import PartitionSpec as P

F32 = jnp.float32
BF = jnp.bfloat16
MESH = pl.DeviceIdType.MESH
EXPERTS = 32
CAP = 40
NEG = 128.0
ANY = pl.BlockSpec(memory_space=pl.ANY)
VM = pl.BlockSpec(memory_space=pltpu.VMEM)
LIMIT = 56 << 20


def dot(a, b):
    return jnp.dot(a, b, preferred_element_type=F32)


def dot_nt(a, b):
    return lax.dot_general(a, b, (((1,), (1,)), ((), ())), preferred_element_type=F32)


def dot_tn(a, b):
    return lax.dot_general(a, b, (((0,), (0,)), ((), ())), preferred_element_type=F32)


def add_low(a, b):
    return (a.astype(F32) + b.astype(F32)).astype(BF)


class Place:
    def __init__(self):
        c = lax.axis_index("ctx")
        f = lax.axis_index("fsdp")
        self.c, self.f = c, f
        self.z, self.xl = c // 2, lax.rem(c, 2)
        self.y, self.xh, self.k = f // 4, lax.rem(f // 2, 2), lax.rem(f, 2)
        self.cx = c + 1 - 2 * self.xl
        self.fx = f + 2 - 4 * self.xh
        self.z_up = (lax.rem(c + 2, 8), f)
        self.z_dn = (lax.rem(c + 6, 8), f)
        self.x_near = (self.cx, f)
        self.y_up = (c, lax.rem(f + 4, 16))
        self.y_dn = (c, lax.rem(f + 12, 16))
        self.x_far = (c, self.fx)
        self.core = (c, f + 1 - 2 * self.k)

    def ctx_peer(self, i):
        return (lax.rem(self.c + i, 8), self.f)

    def fsdp_peer(self, i):
        return (self.c, lax.rem(self.f + i, 16))


class Wire:
    def __init__(self, ssem, rsem):
        self.ssem, self.rsem = ssem, rsem
        self.started = []

    def send(self, src, dst, device):
        n = len(self.started)
        copy = pltpu.make_async_remote_copy(
            src_ref=src,
            dst_ref=dst,
            send_sem=self.ssem.at[n],
            recv_sem=self.rsem.at[n],
            device_id=device,
            device_id_type=MESH,
        )
        copy.start()
        self.started.append(copy)
        return copy

    def done(self):
        for copy in self.started:
            copy.wait_send()


def greet(devices):
    barrier = pltpu.get_barrier_semaphore()
    for device in devices:
        pl.semaphore_signal(barrier, inc=1, device_id=device, device_id_type=MESH)
    pl.semaphore_wait(barrier, len(devices))


def run_all(steps):
    steps = list(steps)
    while steps:
        alive = []
        for step in steps:
            try:
                next(step)
                alive.append(step)
            except StopIteration:
                pass
        steps = alive


def gather16(w, p, own, out, half, local):
    f, fx = p.f, p.fx
    keep = pltpu.make_async_copy(own, out.at[f], local)
    keep.start()
    from_x = w.send(own, out.at[f], p.x_far)
    rings = [(w.send(own, out.at[f], p.y_up), w.send(own, out.at[f], p.y_dn), f)]
    cores = [w.send(own, out.at[f], p.core)]
    yield
    from_x.wait_recv()
    rings.append((w.send(out.at[fx], out.at[fx], p.y_up), w.send(out.at[fx], out.at[fx], p.y_dn), fx))
    cores.append(w.send(out.at[fx], out.at[fx], p.core))
    yield
    halves = []
    for up, down, slot in rings:
        up.wait_recv()
        low = lax.rem(slot + 12, 16)
        part = out.at[low, pl.ds(0, half)]
        halves.append(w.send(part, part, p.y_up))
        cores.append(w.send(out.at[low], out.at[low], p.core))
        down.wait_recv()
        high = lax.rem(slot + 4, 16)
        part = out.at[high, pl.ds(half, own.shape[0] - half)]
        halves.append(w.send(part, part, p.y_dn))
        cores.append(w.send(out.at[high], out.at[high], p.core))
        yield
    for i, slot in ((0, f), (2, fx)):
        halves[i].wait_recv()
        halves[i + 1].wait_recv()
        far = lax.rem(slot + 8, 16)
        cores.append(w.send(out.at[far], out.at[far], p.core))
        yield
    for copy in cores:
        copy.wait_recv()
    keep.wait()


def gather8(w, p, own, out, half, local):
    c, cx = p.c, p.cx
    keep = pltpu.make_async_copy(own, out.at[c], local)
    keep.start()
    from_x = w.send(own, out.at[c], p.x_near)
    rings = [(w.send(own, out.at[c], p.z_up), w.send(own, out.at[c], p.z_dn), c)]
    yield
    from_x.wait_recv()
    rings.append((w.send(out.at[cx], out.at[cx], p.z_up), w.send(out.at[cx], out.at[cx], p.z_dn), cx))
    yield
    halves = []
    for up, down, slot in rings:
        up.wait_recv()
        part = out.at[lax.rem(slot + 6, 8), pl.ds(0, half)]
        halves.append(w.send(part, part, p.z_up))
        down.wait_recv()
        if half < own.shape[0]:
            part = out.at[lax.rem(slot + 2, 8), pl.ds(half, own.shape[0] - half)]
            halves.append(w.send(part, part, p.z_dn))
        yield
    for copy in halves:
        copy.wait_recv()
    keep.wait()


def ring_reduce(w, up, down, mine, far_up, far_down, near_up, near_down):
    a = w.send(mine(2, 0), far_up, up)
    b = w.send(mine(2, 1), far_down, down)
    c = w.send(mine(1, 1), near_up(1), up)
    d = w.send(mine(3, 0), near_down(0), down)
    yield
    a.wait_recv()
    far_up[...] = add_low(mine(1, 0)[...], far_up[...])
    e = w.send(far_up, near_up(0), up)
    b.wait_recv()
    far_down[...] = add_low(mine(3, 1)[...], far_down[...])
    g = w.send(far_down, near_down(1), down)
    yield
    for copy in (c, d, e, g):
        copy.wait_recv()


def reduce16(w, p, part, other, acc, far, near, last, finish):
    rows = part.shape[1]
    half = rows // 2
    order = (2, 1, 3, 0)
    arrivals = []
    for dy in order:
        for e in (0, 1):
            slot = lax.rem((p.f, p.fx)[e] + 4 * dy, 16) + 1 - 2 * p.k
            arrivals.append(w.send(part.at[slot], other.at[dy, e], p.core))
    yield

    def merge(i, dy):
        for e in (0, 1):
            arrivals[2 * i + e].wait_recv()
            slot = lax.rem((p.f, p.fx)[e] + 4 * dy, 16)
            acc[dy, e] = add_low(part[slot], other[dy, e])

    spans = {0: pl.ds(0, half), 1: pl.ds(half, rows - half)}

    def mine(dy, h):
        return acc.at[dy, :, spans[h]]

    for i, dy in enumerate(order[:3]):
        merge(i, dy)
    ring = ring_reduce(
        w,
        p.y_up,
        p.y_dn,
        mine,
        far.at[0],
        far.at[1],
        lambda h: near.at[0, :, spans[h]],
        lambda h: near.at[1, :, spans[h]],
    )
    next(ring)
    merge(3, 0)
    yield
    for _ in ring:
        yield
    theirs = acc[0, 1].astype(F32) + near[0, 1].astype(F32) + near[1, 1].astype(F32)
    acc[0, 1] = theirs.astype(BF)
    copy = w.send(acc.at[0, 1], last, p.x_far)
    yield
    total = acc[0, 0].astype(F32) + near[0, 0].astype(F32) + near[1, 0].astype(F32)
    copy.wait_recv()
    finish(total + last[...].astype(F32))


def reduce16_scratch(rows, cols):
    return [
        pltpu.VMEM((4, 2, rows, cols), BF),
        pltpu.VMEM((4, 2, rows, cols), BF),
        pltpu.VMEM((2, 2, rows // 2, cols), BF),
        pltpu.VMEM((2, 2, rows, cols), BF),
        pltpu.VMEM((rows, cols), BF),
    ]


def remote_params(cid):
    return pltpu.CompilerParams(collective_id=cid, has_side_effects=True, vmem_limit_bytes=LIMIT)


def local_params():
    return pltpu.CompilerParams(vmem_limit_bytes=LIMIT)


def shaped(shape, dtype):
    return jax.ShapeDtypeStruct(shape, dtype)


def first_kernel(x, seg, wp, wo, g, cot, xs, segs, wps, wos, gs, cots, ssem, rsem, local):
    p = Place()
    w = Wire(ssem, rsem)
    greet([p.z_up, p.z_dn, p.x_near, p.y_up, p.y_dn, p.x_far, p.core])
    run_all(
        [
            gather8(w, p, x, xs, 64, local.at[0]),
            gather8(w, p, seg, segs, 8, local.at[1]),
            gather16(w, p, wp, wps, 48, local.at[2]),
            gather16(w, p, wo, wos, 32, local.at[3]),
            gather16(w, p, g, gs, 16, local.at[4]),
            gather16(w, p, cot, cots, 64, local.at[5]),
        ]
    )
    w.done()


def first_gather(x, seg, wp, wo, g, cot):
    return pl.pallas_call(
        first_kernel,
        name="first_gather",
        out_shape=(
            shaped((8,) + x.shape, BF),
            shaped((8,) + seg.shape, jnp.int32),
            shaped((16,) + wp.shape, BF),
            shaped((16,) + wo.shape, BF),
            shaped((16,) + g.shape, F32),
            shaped((16,) + cot.shape, BF),
        ),
        in_specs=[ANY] * 6,
        out_specs=(ANY,) * 6,
        scratch_shapes=[
            pltpu.SemaphoreType.DMA((96,)),
            pltpu.SemaphoreType.DMA((96,)),
            pltpu.SemaphoreType.DMA((6,)),
        ],
        compiler_params=remote_params(1),
    )(x, seg, wp, wo, g, cot)


def lanes(shape):
    return lax.broadcasted_iota(jnp.int32, shape, len(shape) - 1)


def spin(v):
    first = lax.rem(lanes(v.shape), 64) < 32
    return jnp.where(first, pltpu.roll(v, 96, 1), pltpu.roll(v, 32, 1))


def head_sums(v):
    low = lanes(v.shape) < 64
    left = jnp.sum(jnp.where(low, v, 0.0), axis=-1, keepdims=True)
    right = jnp.sum(jnp.where(low, 0.0, v), axis=-1, keepdims=True)
    return jnp.where(low, left, right)


def split3(v):
    high = v.astype(BF).astype(F32)
    rest = v - high
    mid = rest.astype(BF).astype(F32)
    return high, mid, (rest - mid).astype(BF).astype(F32)


def columns3(v, base, shape):
    where = lanes(shape)
    high, mid, low = split3(v)
    return jnp.where(
        where == base, high, jnp.where(where == base + 1, mid, jnp.where(where == base + 2, low, 0.0))
    )


def attend_kernel(
    xs, segs, wps, gain, qk_gain, trig, normed, raw, qx, kx, vx, ctx_full, ctx_low, q_plain
):
    weights = wps[:, 0:64, :].reshape(1024, 256)
    place = lanes((8, 128))
    docs = lax.broadcasted_iota(jnp.int32, (8, 128), 0)
    spot = jnp.where(place == docs + 64, 1.0, 0.0)
    low = lanes((128, 128)) < 64

    def project(b, carry):
        x = xs[b].astype(F32)
        r = lax.rsqrt(jnp.mean(x * x, axis=-1, keepdims=True) + 1e-5)
        n = (x * r * gain[...]).astype(BF)
        normed[b] = n
        qkv = dot(n, weights)
        raw[b] = qkv
        q, kv = qkv[:, 0:128], qkv[:, 128:256]
        cos, sin = trig[0, b], trig[1, b]
        qn = q * lax.rsqrt(head_sums(q * q) * (1.0 / 64) + 1e-6) * qk_gain[0:1]
        q_rot = (qn * cos + spin(qn) * sin).astype(BF).astype(F32) * 0.125
        kn = kv * lax.rsqrt(head_sums(kv * kv) * (1.0 / 64) + 1e-6) * qk_gain[1:2]
        k_rot = kn * cos + spin(kn) * sin
        same = jnp.where(segs[b] == docs, 1.0, 0.0)
        doc = dot_tn(same, spot)
        bias = jnp.where((lanes((128, 128)) >= 64) & (lanes((128, 128)) < 72), (doc - 1.0) * NEG, 0.0)
        ones = jnp.where((lanes((128, 128)) >= 72) & (lanes((128, 128)) < 75), 1.0, 0.0)
        kx[b] = jnp.where(low, k_rot, doc + ones).astype(BF)
        one_v = jnp.where((lanes((128, 128)) >= 64) & (lanes((128, 128)) < 67), 1.0, 0.0)
        vx[b] = jnp.where(low, pltpu.roll(kv, 64, 1), one_v).astype(BF)
        q_plain[0, b] = jnp.where(low, q_rot, bias).astype(BF)
        q_plain[1, b] = jnp.where(low, pltpu.roll(q_rot, 64, 1), bias).astype(BF)
        return carry

    lax.fori_loop(0, 8, project, 0)
    k_all = kx[...].reshape(1024, 128)
    v_all = vx[...].reshape(1024, 128)

    def attend(b, carry):
        out = []
        for h in range(2):
            q = q_plain[h, b]
            e = jnp.exp(dot_nt(q, k_all)).astype(BF)
            o = dot(e, v_all)
            total = o[:, 64:65]
            out.append(o / total)
            keep = jnp.where(lanes((128, 128)) >= 72, 0.0, q.astype(F32))
            qx[h, b] = (keep + columns3(-jnp.log(total), 72, (128, 128))).astype(BF)
        both = jnp.where(low, out[0], pltpu.roll(out[1], 64, 1))
        ctx_full[b] = both
        ctx_low[b] = both.astype(BF)
        return carry

    lax.fori_loop(0, 8, attend, 0)


def attend(xs, segs, wps, gain, qk_gain, trig):
    return pl.pallas_call(
        attend_kernel,
        name="attend",
        out_shape=(
            shaped((8, 128, 1024), BF),
            shaped((8, 128, 256), F32),
            shaped((2, 8, 128, 128), BF),
            shaped((8, 128, 128), BF),
            shaped((8, 128, 128), BF),
            shaped((8, 128, 128), F32),
            shaped((8, 128, 128), BF),
        ),
        in_specs=[VM] * 6,
        out_specs=(VM,) * 7,
        scratch_shapes=[pltpu.VMEM((2, 8, 128, 128), BF)],
        compiler_params=local_params(),
    )(xs, segs, wps, gain, qk_gain, trig)


def middle_kernel(ctx, x, wos, gain, middle, ctx_rows, mids, rows, own, ssem, rsem, local):
    p = Place()
    w = Wire(ssem, rsem)
    greet([p.ctx_peer(i) for i in range(1, 8)] + [p.y_up, p.y_dn, p.x_far, p.core])
    place = pl.ds(pl.multiple_of(p.c * 128, 128), 128)
    keep = pltpu.make_async_copy(ctx.at[p.c], rows.at[:, place], local.at[0])
    keep.start()
    arrivals = []
    for i in range(1, 8):
        to = lax.rem(p.c + i, 8)
        arrivals.append(w.send(ctx.at[to], rows.at[:, place], (to, p.f)))
    keep.wait()
    for copy in arrivals:
        copy.wait_recv()
    for t in range(4):
        cols = slice(256 * t, 256 * t + 256)
        middle[:, cols] = x[:, cols].astype(F32) + dot(rows[...], wos[:, cols])
    m = middle[...]
    r = lax.rsqrt(jnp.mean(m * m, axis=-1, keepdims=True) + 1e-5)
    own[...] = (m * r * gain[...]).astype(BF)
    ctx_rows[...] = rows[...]
    run_all([gather16(w, p, own, mids, 64, local.at[1])])
    w.done()


def middle_gather(ctx, x, wos, gain):
    return pl.pallas_call(
        middle_kernel,
        name="middle_gather",
        out_shape=(
            shaped((128, 1024), F32),
            shaped((128, 1024), BF),
            shaped((16, 128, 1024), BF),
        ),
        in_specs=[ANY, VM, VM, VM],
        out_specs=(VM, VM, ANY),
        scratch_shapes=[
            pltpu.VMEM((128, 1024), BF),
            pltpu.VMEM((128, 1024), BF),
            pltpu.SemaphoreType.DMA((32,)),
            pltpu.SemaphoreType.DMA((32,)),
            pltpu.SemaphoreType.DMA((2,)),
        ],
        compiler_params=remote_params(2),
    )(ctx, x, wos, gain)


def expert_kernel(
    gs, mids, cots, wg, wu, wd,
    outs, grads, dg, du, dd,
    table, key, hot, xin, gout, gate, act, ggp, gup, yo, yi,
):
    f = lax.axis_index("fsdp")
    for s in range(16):
        table[2 * s : 2 * s + 2, :] = gs[s, pl.ds(2 * f, 2), :]
    named = table[...] > 0.0
    row = lax.broadcasted_iota(jnp.int32, (128, 128), 0)
    col = lax.broadcasted_iota(jnp.int32, (128, 128), 1)
    before = jnp.where(row < col, 1.0, 0.0).astype(BF)
    count = dot(jnp.where(named, 1.0, 0.0).astype(BF), before)
    odd = lax.rem(lax.broadcasted_iota(jnp.int32, (32, 128), 0) // 2, 2).astype(F32)
    key[...] = jnp.where(named, count + odd * CAP, -1.0)
    slot = lax.broadcasted_iota(jnp.int32, (2 * CAP, 256), 0).astype(F32)

    for q in range(8):
        pair = mids[2 * q : 2 * q + 2].reshape(256, 1024)
        cot = cots[2 * q : 2 * q + 2].reshape(256, 1024)
        rows = slice(2 * CAP * q, 2 * CAP * q + 2 * CAP)
        for j in range(2):
            a, b = 4 * q + j, 4 * q + 2 + j
            keys = jnp.concatenate([key[a : a + 1, :], key[b : b + 1, :]], axis=1)
            vals = jnp.concatenate([table[a : a + 1, :], table[b : b + 1, :]], axis=1)
            chosen = slot == keys
            hot[q, j] = jnp.where(chosen, 1.0, 0.0).astype(BF)
            weight = jnp.sum(jnp.where(chosen, vals, 0.0), axis=1, keepdims=True)
            gate[j, rows, :] = jnp.broadcast_to(weight, (2 * CAP, 128))
            xin[j, rows, :] = dot(hot[q, j], pair).astype(BF)
            gout[j, rows, :] = (weight * dot(hot[q, j], cot)).astype(BF)

    for j in range(2):

        def rows_step(t, carry, j=j):
            rows = pl.ds(pl.multiple_of(t * 128, 128), 128)
            x = xin[j, rows, :]
            go = gout[j, rows, :]
            gp = dot(x, wg[j])
            up = dot(x, wu[j])
            s = 1.0 / (1.0 + jnp.exp(-gp))
            silu = gp * s
            a = (silu * up).astype(BF)
            act[rows, :] = a
            eo = dot(a, wd[j])
            yo[j, rows, :] = (gate[j, rows, 0:1] * eo).astype(BF)
            ga = dot_nt(go, wd[j])
            gg = (ga * up * (s * (1.0 + gp * (1.0 - s)))).astype(BF)
            gu = (ga * silu).astype(BF)
            ggp[rows, :] = gg
            gup[rows, :] = gu
            yi[j, rows, :] = (dot_nt(gg, wg[j]) + dot_nt(gu, wu[j])).astype(BF)
            return carry

        lax.fori_loop(0, 5, rows_step, 0)

        def grads_step(t, carry, j=j):
            cols = pl.ds(pl.multiple_of(t * 256, 256), 256)
            x = xin[j, :, cols]
            dg[j, cols, :] = dot_tn(x, ggp[...]).astype(BF)
            du[j, cols, :] = dot_tn(x, gup[...]).astype(BF)
            dd[j, :, cols] = dot_tn(act[...], gout[j, :, cols]).astype(BF)
            return carry

        lax.fori_loop(0, 4, grads_step, 0)

    for q in range(8):
        rows = slice(2 * CAP * q, 2 * CAP * q + 2 * CAP)
        o = dot_tn(hot[q, 0], yo[0, rows, :]) + dot_tn(hot[q, 1], yo[1, rows, :])
        outs[2 * q : 2 * q + 2] = o.astype(BF).reshape(2, 128, 1024)
        g = dot_tn(hot[q, 0], yi[0, rows, :]) + dot_tn(hot[q, 1], yi[1, rows, :])
        grads[2 * q : 2 * q + 2] = g.astype(BF).reshape(2, 128, 1024)


def experts(gs, mids, cots, wg, wu, wd):
    slots = 16 * CAP
    return pl.pallas_call(
        expert_kernel,
        name="experts",
        out_shape=(
            shaped((16, 128, 1024), BF),
            shaped((16, 128, 1024), BF),
            shaped((2, 1024, 512), BF),
            shaped((2, 1024, 512), BF),
            shaped((2, 512, 1024), BF),
        ),
        in_specs=[VM] * 6,
        out_specs=(VM,) * 5,
        scratch_shapes=[
            pltpu.VMEM((32, 128), F32),
            pltpu.VMEM((32, 128), F32),
            pltpu.VMEM((8, 2, 2 * CAP, 256), BF),
            pltpu.VMEM((2, slots, 1024), BF),
            pltpu.VMEM((2, slots, 1024), BF),
            pltpu.VMEM((2, slots, 128), F32),
            pltpu.VMEM((slots, 512), BF),
            pltpu.VMEM((slots, 512), BF),
            pltpu.VMEM((slots, 512), BF),
            pltpu.VMEM((2, slots, 1024), BF),
            pltpu.VMEM((2, slots, 1024), BF),
        ],
        compiler_params=local_params(),
    )(gs, mids, cots, wg, wu, wd)


def return_kernel(
    grads, outs, dg, du, dd, middle, cot, wos, gain, ctx_rows,
    output, grad_middle, grad_gain, dctx, grad_out, own_g, own_u, own_d,
    go, ga, gf, gn, gl, oo, oa, of, on, ol,
    gfar, gnear, gx, ufar, unear, ux, dmine, dx, dfar, dnear,
    total, branch, back, ssem, rsem, local,
):
    p = Place()
    w = Wire(ssem, rsem)
    greet(
        [p.ctx_peer(i) for i in range(1, 8)]
        + [p.y_up, p.y_dn, p.x_far, p.core]
    )

    def keep_total(v):
        total[...] = v

    def write_output(v):
        output[...] = (middle[...] + v).astype(BF)

    def side(ref, far, near, last, own):
        def mine(d, h):
            start = lax.rem(p.z + d, 4) * 256
            return ref.at[:, pl.ds(pl.multiple_of(start + 128 * h, 128), 128)]

        spans = (pl.ds(0, 128), pl.ds(128, 128))
        yield from ring_reduce(
            w,
            p.z_up,
            p.z_dn,
            mine,
            far.at[0],
            far.at[1],
            lambda h: near.at[0, :, spans[h]],
            lambda h: near.at[1, :, spans[h]],
        )
        block = pl.ds(pl.multiple_of(p.z * 256, 256), 256)

        def summed(e):
            return (
                ref[e, block].astype(F32) + near[0, e].astype(F32) + near[1, e].astype(F32)
            )

        near[0, 1 - p.xl] = summed(1 - p.xl).astype(BF)
        copy = w.send(near.at[0, 1 - p.xl], last, p.x_near)
        yield
        mine_now = summed(p.xl)
        copy.wait_recv()
        own[...] = (mine_now + last[...].astype(F32)).astype(BF)

    def down():
        copy = w.send(dd.at[1 - p.xl], dx, p.x_near)
        yield
        copy.wait_recv()
        dmine[...] = add_low(dd[p.xl], dx[...])

        def mine(d, h):
            start = lax.rem(p.z + d, 4) * 128
            return dmine.at[pl.ds(pl.multiple_of(start + 64 * h, 64), 64)]

        spans = (pl.ds(0, 64), pl.ds(64, 64))
        yield from ring_reduce(
            w,
            p.z_up,
            p.z_dn,
            mine,
            dfar.at[0],
            dfar.at[1],
            lambda h: dnear.at[0, spans[h]],
            lambda h: dnear.at[1, spans[h]],
        )
        block = dmine[pl.ds(pl.multiple_of(p.z * 128, 128), 128)].astype(F32)
        own_d[...] = (block + dnear[0].astype(F32) + dnear[1].astype(F32)).astype(BF)

    def tail():
        yield from reduce16(w, p, grads, go, ga, gf, gn, gl, keep_total)
        yield
        m = middle[...]
        gm = total[...] * gain[...]
        r = lax.rsqrt(jnp.mean(m * m, axis=-1, keepdims=True) + 1e-5)
        inner = jnp.mean(gm * m, axis=-1, keepdims=True)
        gmid = cot[...].astype(F32) + r * gm - m * (r * r * r * inner)
        grad_middle[...] = gmid
        grad_gain[...] = jnp.broadcast_to(
            jnp.sum(total[...] * (m * r), axis=0, keepdims=True), (8, 1024)
        )
        branch[...] = gmid.astype(BF)
        for t in range(4):
            cols = slice(256 * t, 256 * t + 256)
            back[:, cols] = dot_nt(branch[...], wos[cols, :]).astype(BF)
        place = pl.ds(pl.multiple_of(p.c * 128, 128), 128)
        keep = pltpu.make_async_copy(back.at[:, place], dctx.at[p.c], local)
        keep.start()
        arrivals = []
        for i in range(1, 8):
            to = lax.rem(p.c + i, 8)
            block = pl.ds(pl.multiple_of(to * 128, 128), 128)
            arrivals.append(w.send(back.at[:, block], dctx.at[p.c], (to, p.f)))
        yield
        for t in range(16):
            rows = slice(64 * t, 64 * t + 64)
            if t % 2 == 0:
                two = dot_tn(ctx_rows[:, 64 * t : 64 * t + 128], branch[...]).astype(BF)
                grad_out[t] = two[0:64]
                grad_out[t + 1] = two[64:128]
        for copy in arrivals:
            copy.wait_recv()
        keep.wait()

    run_all(
        [
            tail(),
            side(dg, gfar, gnear, gx, own_g),
            side(du, ufar, unear, ux, own_u),
            down(),
            reduce16(w, p, outs, oo, oa, of, on, ol, write_output),
        ]
    )
    w.done()


def return_reduce(grads, outs, dg, du, dd, middle, cot, wos, gain, ctx_rows):
    def side():
        return [
            pltpu.VMEM((2, 2, 128, 512), BF),
            pltpu.VMEM((2, 2, 256, 512), BF),
            pltpu.VMEM((256, 512), BF),
        ]

    return pl.pallas_call(
        return_kernel,
        name="return_reduce",
        out_shape=(
            shaped((128, 1024), BF),
            shaped((128, 1024), F32),
            shaped((8, 1024), F32),
            shaped((8, 128, 128), BF),
            shaped((16, 64, 1024), BF),
            shaped((256, 512), BF),
            shaped((256, 512), BF),
            shaped((128, 1024), BF),
        ),
        in_specs=[VM] * 10,
        out_specs=(VM, VM, VM, ANY, VM, VM, VM, VM),
        scratch_shapes=reduce16_scratch(128, 1024)
        + reduce16_scratch(128, 1024)
        + side()
        + side()
        + [
            pltpu.VMEM((512, 1024), BF),
            pltpu.VMEM((512, 1024), BF),
            pltpu.VMEM((2, 64, 1024), BF),
            pltpu.VMEM((2, 128, 1024), BF),
            pltpu.VMEM((128, 1024), F32),
            pltpu.VMEM((128, 1024), BF),
            pltpu.VMEM((128, 1024), BF),
            pltpu.SemaphoreType.DMA((96,)),
            pltpu.SemaphoreType.DMA((96,)),
            pltpu.SemaphoreType.DMA,
        ],
        compiler_params=remote_params(3),
    )(grads, outs, dg, du, dd, middle, cot, wos, gain, ctx_rows)


def backward_kernel(
    dctx, ctx_full, qx, kx, vx, raw, normed, xs, wps, qk_gain, trig,
    partial, grad_w, grad_norm, grad_gains,
    gx, dq, dk, dv, dqkv,
):
    low = lanes((128, 128)) < 64

    def prepare(b, carry):
        d = dctx[b].astype(F32)
        prod = d * ctx_full[b]
        left = jnp.sum(jnp.where(low, prod, 0.0), axis=-1, keepdims=True)
        right = jnp.sum(jnp.where(low, 0.0, prod), axis=-1, keepdims=True)
        gx[0, b] = jnp.where(low, d, columns3(-left, 64, (128, 128))).astype(BF)
        gx[1, b] = jnp.where(
            low, pltpu.roll(d, 64, 1), columns3(-right, 64, (128, 128))
        ).astype(BF)
        return carry

    lax.fori_loop(0, 8, prepare, 0)
    dq[...] = jnp.zeros(dq.shape, F32)

    def block(b, carry):
        k = kx[b]
        v = vx[b]
        grad_k = jnp.zeros((128, 128), F32)
        grad_v = jnp.zeros((128, 128), F32)
        for h in range(2):
            q_all = qx[h].reshape(1024, 128)
            g_all = gx[h].reshape(1024, 128)
            pt = jnp.exp(dot_nt(k, q_all))
            dst = (pt * dot_nt(v, g_all)).astype(BF)
            grad_v = grad_v + dot(pt.astype(BF), g_all)
            grad_k = grad_k + dot(dst, q_all)
            dq[h] += dot_tn(dst, k)
        dk[b] = grad_k
        dv[b] = grad_v
        return carry

    lax.fori_loop(0, 8, block, 0)

    weights = wps[:, 0:64, :].reshape(1024, 256)

    def finish(b, carry):
        norm_sum, q_sum, k_sum = carry
        rows = pl.ds(pl.multiple_of(b * 128, 128), 128)
        cos, sin = trig[0, b], trig[1, b]
        gq = jnp.where(low, dq[0, rows, :], pltpu.roll(dq[1, rows, :], 64, 1)) * 0.125
        gq = gq.astype(BF).astype(F32)
        gkv = jnp.where(low, dk[b], pltpu.roll(dv[b], 64, 1)).astype(BF).astype(F32)
        gq = gq * cos - spin(gq) * sin
        gkv_rot = gkv * cos - spin(gkv) * sin
        q, kv = raw[b, :, 0:128], raw[b, :, 128:256]
        rq = lax.rsqrt(head_sums(q * q) * (1.0 / 64) + 1e-6)
        rk = lax.rsqrt(head_sums(kv * kv) * (1.0 / 64) + 1e-6)
        q_sum = q_sum + jnp.sum(gq * q * rq, axis=0, keepdims=True)
        k_sum = k_sum + jnp.sum(gkv_rot * kv * rk, axis=0, keepdims=True)
        gq = gq * qk_gain[0:1]
        gk = gkv_rot * qk_gain[1:2]
        gq = rq * gq - q * (rq * rq * rq) * (head_sums(gq * q) * (1.0 / 64))
        gk = rk * gk - kv * (rk * rk * rk) * (head_sums(gk * kv) * (1.0 / 64))
        gkv = jnp.where(low, gk, gkv)
        dqkv[rows, 0:128] = gq.astype(BF)
        dqkv[rows, 128:256] = gkv.astype(BF)
        gn = dot_nt(dqkv[rows, :], weights)
        partial[b] = gn.astype(BF)
        x = xs[b].astype(F32)
        r = lax.rsqrt(jnp.mean(x * x, axis=-1, keepdims=True) + 1e-5)
        norm_sum = norm_sum + jnp.sum(gn * (x * r), axis=0, keepdims=True)
        return norm_sum, q_sum, k_sum

    zero = jnp.zeros((1, 128), F32)
    norm_sum, q_sum, k_sum = lax.fori_loop(
        0, 8, finish, (jnp.zeros((1, 1024), F32), zero, zero)
    )
    grad_norm[...] = jnp.broadcast_to(norm_sum, (8, 1024))
    low1 = lanes((1, 128)) < 64
    q_sum = q_sum + pltpu.roll(q_sum, 64, 1)
    grad_gains[...] = jnp.broadcast_to(jnp.where(low1, q_sum, pltpu.roll(k_sum, 64, 1)), (8, 128))
    for t in range(4):
        part = dot_tn(normed[:, :, 256 * t : 256 * t + 256].reshape(1024, 256), dqkv[...])
        grad_w[4 * t : 4 * t + 4] = part.astype(BF).reshape(4, 64, 256)


def attend_back(dctx, ctx_full, qx, kx, vx, raw, normed, xs, wps, qk_gain, trig):
    return pl.pallas_call(
        backward_kernel,
        name="attend_back",
        out_shape=(
            shaped((8, 128, 1024), BF),
            shaped((16, 64, 256), BF),
            shaped((8, 1024), F32),
            shaped((8, 128), F32),
        ),
        in_specs=[VM] * 11,
        out_specs=(VM,) * 4,
        scratch_shapes=[
            pltpu.VMEM((2, 8, 128, 128), BF),
            pltpu.VMEM((2, 1024, 128), F32),
            pltpu.VMEM((8, 128, 128), F32),
            pltpu.VMEM((8, 128, 128), F32),
            pltpu.VMEM((1024, 256), BF),
        ],
        compiler_params=local_params(),
    )(dctx, ctx_full, qx, kx, vx, raw, normed, xs, wps, qk_gain, trig)


def last_kernel(
    partial, grad_w, grad_out, small, own_g, own_u, own_d, x, grad_middle, gain,
    input_grad, w_all, out_all, small_sum, dg, du, dd,
    wo_, wa, wf, wn, wl, oo, oa, of, on, ol,
    xr, acc, zfar, znear, w_own, out_own, out_parts, out_mine, ctx_small, mid_small, fsdp_small,
    total, ssem, rsem, local,
):
    p = Place()
    w = Wire(ssem, rsem)
    greet(
        [p.ctx_peer(i) for i in range(1, 8)]
        + [p.fsdp_peer(i) for i in range(1, 16)]
    )

    def tokens():
        def mine(d, h):
            start = lax.rem(p.z + d, 4) * 2
            return partial.at[pl.ds(start, 2), pl.ds(64 * h, 64)]

        spans = (pl.ds(0, 64), pl.ds(64, 64))
        yield from ring_reduce(
            w,
            p.z_up,
            p.z_dn,
            mine,
            zfar.at[0],
            zfar.at[1],
            lambda h: znear.at[0, :, spans[h]],
            lambda h: znear.at[1, :, spans[h]],
        )

        def summed(e):
            return (
                partial[2 * p.z + e].astype(F32) + znear[0, e].astype(F32) + znear[1, e].astype(F32)
            )

        acc[...] = summed(1 - p.xl).astype(BF)
        copy = w.send(acc, xr, p.x_near)
        yield
        total[...] = summed(p.xl)
        copy.wait_recv()
        gy = (total[...] + xr[...].astype(F32)) * gain[...]
        v = x[...].astype(F32)
        r = lax.rsqrt(jnp.mean(v * v, axis=-1, keepdims=True) + 1e-5)
        inner = jnp.mean(gy * v, axis=-1, keepdims=True)
        input_grad[...] = grad_middle[...] + r * gy - v * (r * r * r * inner)

    def projections():
        def finish(v):
            w_own[...] = v.astype(BF)

        yield from reduce16(w, p, grad_w, wo_, wa, wf, wn, wl, finish)
        yield
        yield from gather8(w, p, w_own, w_all, 32, local.at[0])

    def out_weight():
        def finish(v):
            for i in range(8):
                out_own[i] = v[:, 128 * i : 128 * i + 128].astype(BF)

        yield from reduce16(w, p, grad_out, oo, oa, of, on, ol, finish)
        arrivals = []
        for i in range(1, 8):
            to = lax.rem(p.c + i, 8)
            arrivals.append(w.send(out_own.at[to], out_parts.at[i - 1], (to, p.f)))
        yield
        sums = out_own[p.c].astype(F32)
        for i, copy in enumerate(arrivals):
            copy.wait_recv()
            sums = sums + out_parts[i].astype(F32)
        out_mine[...] = sums.astype(BF)
        yield
        yield from gather8(w, p, out_mine, out_all, 32, local.at[1])

    def vectors():
        first = [
            w.send(small, ctx_small.at[i - 1], p.ctx_peer(i)) for i in range(1, 8)
        ]
        yield
        sums = small[...]
        for i, copy in enumerate(first):
            copy.wait_recv()
            sums = sums + ctx_small[i]
        mid_small[...] = sums
        second = [
            w.send(mid_small, fsdp_small.at[p.f], p.fsdp_peer(i)) for i in range(1, 16)
        ]
        fsdp_small[p.f] = sums
        yield
        for copy in second:
            copy.wait_recv()
        sums = fsdp_small[0]
        for i in range(1, 16):
            sums = sums + fsdp_small[i]
        small_sum[...] = sums

    def side(own, out, sem):
        def block(dz, e=None):
            rows = pl.ds(pl.multiple_of(lax.rem(p.z + dz, 4) * 256, 256), 256)
            return out.at[:, rows] if e is None else out.at[e, rows]

        def half(dz, h):
            start = lax.rem(p.z + dz, 4) * 256 + 128 * h
            return out.at[:, pl.ds(pl.multiple_of(start, 128), 128)]

        keep = pltpu.make_async_copy(own, block(0, p.xl), sem)
        keep.start()
        a = w.send(own, block(0, p.xl), p.x_near)
        yield
        keep.wait()
        a.wait_recv()
        up = w.send(block(0), block(0), p.z_up)
        down = w.send(block(0), block(0), p.z_dn)
        yield
        up.wait_recv()
        c = w.send(half(3, 0), half(3, 0), p.z_up)
        down.wait_recv()
        d = w.send(half(1, 1), half(1, 1), p.z_dn)
        yield
        c.wait_recv()
        d.wait_recv()

    def downs():
        def block(dz):
            return dd.at[p.xl, pl.ds(pl.multiple_of(lax.rem(p.z + dz, 4) * 128, 128), 128)]

        def half(dz, h):
            start = lax.rem(p.z + dz, 4) * 128 + 64 * h
            return dd.at[p.xl, pl.ds(pl.multiple_of(start, 64), 64)]

        keep = pltpu.make_async_copy(own_d, block(0), local.at[4])
        keep.start()
        up = w.send(own_d, block(0), p.z_up)
        down = w.send(own_d, block(0), p.z_dn)
        near = [w.send(own_d, block(0), p.x_near)]
        yield
        up.wait_recv()
        c = w.send(half(3, 0), half(3, 0), p.z_up)
        near.append(w.send(block(3), block(3), p.x_near))
        down.wait_recv()
        d = w.send(half(1, 1), half(1, 1), p.z_dn)
        near.append(w.send(block(1), block(1), p.x_near))
        yield
        c.wait_recv()
        d.wait_recv()
        near.append(w.send(block(2), block(2), p.x_near))
        yield
        for copy in near:
            copy.wait_recv()
        keep.wait()

    run_all(
        [
            tokens(),
            vectors(),
            projections(),
            out_weight(),
            side(own_g, dg, local.at[2]),
            side(own_u, du, local.at[3]),
            downs(),
        ]
    )
    w.done()


def last_reduce(partial, grad_w, grad_out, small, own_g, own_u, own_d, x, grad_middle, gain):
    return pl.pallas_call(
        last_kernel,
        name="last_reduce",
        out_shape=(
            shaped((128, 1024), F32),
            shaped((8, 64, 256), BF),
            shaped((8, 64, 128), BF),
            shaped(small.shape, F32),
            shaped((2, 1024, 512), BF),
            shaped((2, 1024, 512), BF),
            shaped((2, 512, 1024), BF),
        ),
        in_specs=[VM] * 10,
        out_specs=(VM, ANY, ANY, VM, ANY, ANY, ANY),
        scratch_shapes=reduce16_scratch(64, 256)
        + reduce16_scratch(64, 1024)
        + [
            pltpu.VMEM((128, 1024), BF),
            pltpu.VMEM((128, 1024), BF),
            pltpu.VMEM((2, 2, 64, 1024), BF),
            pltpu.VMEM((2, 2, 128, 1024), BF),
            pltpu.VMEM((64, 256), BF),
            pltpu.VMEM((8, 64, 128), BF),
            pltpu.VMEM((7, 64, 128), BF),
            pltpu.VMEM((64, 128), BF),
            pltpu.VMEM((7,) + small.shape, F32),
            pltpu.VMEM(small.shape, F32),
            pltpu.VMEM((16,) + small.shape, F32),
            pltpu.VMEM((128, 1024), F32),
            pltpu.SemaphoreType.DMA((128,)),
            pltpu.SemaphoreType.DMA((128,)),
            pltpu.SemaphoreType.DMA((5,)),
        ],
        compiler_params=remote_params(4),
    )(partial, grad_w, grad_out, small, own_g, own_u, own_d, x, grad_middle, gain)


def trig_tables():
    index = np.arange(1024)
    stored = index // 64
    natural = np.where(stored % 2 == 0, stored // 2, 15 - stored // 2)
    pos = (natural * 64 + index % 64).astype(np.float32)
    freq = (10000.0 ** (-np.arange(32) * 2.0 / 64)).astype(np.float32)
    angle = (pos[:, None] * freq[None, :]).astype(np.float64)
    cos, sin = np.cos(angle), np.sin(angle)
    cos = np.concatenate([cos] * 4, axis=1)
    sin = np.concatenate([-sin, sin, -sin, sin], axis=1)
    return np.stack([cos, sin]).astype(np.float32).reshape(2, 8, 128, 128)


def on_device(
    inputs, segments, routes, gate_weights, cotangent, norm_in, norm_mid, q_gain, k_gain,
    w_query, w_key, w_value, w_out, w_gate, w_up, w_down,
):
    c = lax.axis_index("ctx")
    f = lax.axis_index("fsdp")
    x, cot = inputs[0], cotangent[0]
    trig = jnp.asarray(trig_tables())
    wp = jnp.concatenate(
        [
            lax.dynamic_slice(w_query, (0, 128 * c), (64, 128)),
            lax.dynamic_slice(w_key, (0, 64 * c), (64, 64)),
            lax.dynamic_slice(w_value, (0, 64 * c), (64, 64)),
        ],
        axis=1,
    )
    gains = jnp.pad(jnp.concatenate([norm_in, norm_mid])[None], ((0, 15), (0, 128)))
    wp = jnp.concatenate([wp, gains], axis=0)
    seg = jnp.broadcast_to(segments, (8, 128))
    expert_ids = jnp.arange(EXPERTS, dtype=jnp.int32)
    g = jnp.sum(
        jnp.where(
            routes[0].T[None, :, :] == expert_ids[:, None, None], gate_weights[0].T[None], 0.0
        ),
        axis=1,
    )
    ones = jnp.ones((64,), F32)
    qk_gain = jnp.stack(
        [
            jnp.concatenate([q_gain, q_gain]).astype(F32),
            jnp.concatenate([k_gain.astype(F32), ones]),
        ]
    )
    xs, segs, wps, wos, gs, cots = first_gather(x, seg, wp, w_out, g, cot)
    gain_in = wps[:, 64, 0:64].reshape(1, 1024).astype(F32)
    gain_mid = wps[:, 64, 64:128].reshape(1, 1024).astype(F32)
    wo_full = wos.reshape(1024, 1024)
    normed, raw, qx, kx, vx, ctx_full, ctx_low = attend(xs, segs, wps, gain_in, qk_gain, trig)
    middle, ctx_rows, mids = middle_gather(ctx_low, x, wo_full, gain_mid)
    outs, grads, dg, du, dd = experts(gs, mids, cots, w_gate, w_up, w_down)
    output, grad_middle, grad_gain_mid, dctx, grad_out, own_g, own_u, own_d = return_reduce(
        grads, outs, dg, du, dd, middle, cot, wo_full, gain_mid, ctx_rows
    )
    partial, grad_w, grad_gain_in, grad_gains = attend_back(
        dctx, ctx_full, qx, kx, vx, raw, normed, xs, wps, qk_gain, trig
    )
    small = jnp.concatenate(
        [
            grad_gain_in[0].reshape(8, 128),
            grad_gain_mid[0].reshape(8, 128),
            grad_gains,
        ]
    )
    input_grad, w_all, out_all, small_sum, dg, du, dd = last_reduce(
        partial, grad_w, grad_out, small, own_g, own_u, own_d, x, grad_middle, gain_in
    )
    grad_wq = w_all[:, :, 0:128].transpose(1, 0, 2).reshape(64, 1024).astype(F32)
    grad_wk = w_all[:, :, 128:192].transpose(1, 0, 2).reshape(64, 512).astype(F32)
    grad_wv = w_all[:, :, 192:256].transpose(1, 0, 2).reshape(64, 512).astype(F32)
    grad_wo = out_all.transpose(1, 0, 2).reshape(64, 1024).astype(F32)
    grad_norm_in = lax.dynamic_slice(small_sum[0:8].reshape(1024), (64 * f,), (64,))
    grad_norm_mid = lax.dynamic_slice(small_sum[8:16].reshape(1024), (64 * f,), (64,))
    return (
        output[None],
        input_grad[None],
        grad_norm_in,
        grad_norm_mid,
        small_sum[16, 0:64],
        small_sum[16, 64:128],
        grad_wq,
        grad_wk,
        grad_wv,
        grad_wo,
        dg.astype(F32),
        du.astype(F32),
        dd.astype(F32),
    )


def solution(mesh):
    rows = P("fsdp", "ctx", None)
    in_specs = (
        rows,
        P("fsdp", "ctx"),
        rows,
        rows,
        rows,
        P("fsdp"),
        P("fsdp"),
        P(),
        P(),
        P("fsdp", None),
        P("fsdp", None),
        P("fsdp", None),
        P("fsdp", None),
        P("fsdp", None, None),
        P("fsdp", None, None),
        P("fsdp", None, None),
    )
    out_specs = (
        rows,
        rows,
        P("fsdp"),
        P("fsdp"),
        P(),
        P(),
        P("fsdp", None),
        P("fsdp", None),
        P("fsdp", None),
        P("fsdp", None),
        P("fsdp", None, None),
        P("fsdp", None, None),
        P("fsdp", None, None),
    )
    return jax.shard_map(
        on_device, mesh=mesh, in_specs=in_specs, out_specs=out_specs, check_vma=False
    )
```

```python
from types import SimpleNamespace

import jax
import jax.numpy as jnp
import numpy as np
from jax import lax
from jax.experimental import pallas as pl
from jax.experimental.pallas import tpu as pltpu
from jax.sharding import PartitionSpec as P

F32 = jnp.float32
BF = jnp.bfloat16
MESH = pl.DeviceIdType.MESH
EXPERTS = 32
CAP = 40
NEG = 128.0
ANY = pl.BlockSpec(memory_space=pl.ANY)
VM = pl.BlockSpec(memory_space=pltpu.VMEM)
LIMIT = 62 << 20


def dot(a, b):
    return jnp.dot(a, b, preferred_element_type=F32)


def dot_nt(a, b):
    return lax.dot_general(a, b, (((1,), (1,)), ((), ())), preferred_element_type=F32)


def dot_tn(a, b):
    return lax.dot_general(a, b, (((0,), (0,)), ((), ())), preferred_element_type=F32)


def add_low(a, b):
    return (a.astype(F32) + b.astype(F32)).astype(BF)


class Place:
    def __init__(self):
        c = lax.axis_index("ctx")
        f = lax.axis_index("fsdp")
        self.c, self.f = c, f
        self.z, self.xl = c // 2, lax.rem(c, 2)
        self.y, self.xh, self.k = f // 4, lax.rem(f // 2, 2), lax.rem(f, 2)
        self.cx = c + 1 - 2 * self.xl
        self.fx = f + 2 - 4 * self.xh
        self.z_up = (lax.rem(c + 2, 8), f)
        self.z_dn = (lax.rem(c + 6, 8), f)
        self.x_near = (self.cx, f)
        self.y_up = (c, lax.rem(f + 4, 16))
        self.y_dn = (c, lax.rem(f + 12, 16))
        self.x_far = (c, self.fx)
        self.core = (c, f + 1 - 2 * self.k)

    def ctx_peer(self, i):
        return (lax.rem(self.c + i, 8), self.f)

    def fsdp_peer(self, i):
        return (self.c, lax.rem(self.f + i, 16))


class Wire:
    def __init__(self, ssem, rsem):
        self.ssem, self.rsem = ssem, rsem
        self.started = []

    def send(self, src, dst, device):
        n = len(self.started)
        copy = pltpu.make_async_remote_copy(
            src_ref=src,
            dst_ref=dst,
            send_sem=self.ssem.at[n],
            recv_sem=self.rsem.at[n],
            device_id=device,
            device_id_type=MESH,
        )
        copy.start()
        self.started.append(copy)
        return copy

    def done(self):
        for copy in self.started:
            copy.wait_send()


def greet(devices):
    barrier = pltpu.get_barrier_semaphore()
    for device in devices:
        pl.semaphore_signal(barrier, inc=1, device_id=device, device_id_type=MESH)
    return lambda: pl.semaphore_wait(barrier, len(devices))


class Fetch:
    def __init__(self, sem):
        self.sem, self.n, self.live = sem, 0, {}

    def go(self, name, src, dst):
        copy = pltpu.make_async_copy(src, dst, self.sem.at[self.n])
        copy.start()
        self.n += 1
        self.live.setdefault(name, []).append(copy)

    def need(self, *names):
        for name in names:
            for copy in self.live.pop(name, []):
                copy.wait()


def run_all(steps):
    steps = list(steps)
    while steps:
        alive = []
        for step in steps:
            try:
                next(step)
                alive.append(step)
            except StopIteration:
                pass
        steps = alive


def gather16(w, p, own, out, half, local):
    f, fx = p.f, p.fx
    keep = pltpu.make_async_copy(own, out.at[f], local)
    keep.start()
    from_x = w.send(own, out.at[f], p.x_far)
    rings = [(w.send(own, out.at[f], p.y_up), w.send(own, out.at[f], p.y_dn), f)]
    cores = [w.send(own, out.at[f], p.core)]
    yield
    from_x.wait_recv()
    rings.append((w.send(out.at[fx], out.at[fx], p.y_up), w.send(out.at[fx], out.at[fx], p.y_dn), fx))
    cores.append(w.send(out.at[fx], out.at[fx], p.core))
    yield
    halves = []
    for up, down, slot in rings:
        up.wait_recv()
        low = lax.rem(slot + 12, 16)
        part = out.at[low, pl.ds(0, half)]
        halves.append(w.send(part, part, p.y_up))
        cores.append(w.send(out.at[low], out.at[low], p.core))
        down.wait_recv()
        high = lax.rem(slot + 4, 16)
        part = out.at[high, pl.ds(half, own.shape[0] - half)]
        halves.append(w.send(part, part, p.y_dn))
        cores.append(w.send(out.at[high], out.at[high], p.core))
        yield
    for i, slot in ((0, f), (2, fx)):
        halves[i].wait_recv()
        halves[i + 1].wait_recv()
        far = lax.rem(slot + 8, 16)
        cores.append(w.send(out.at[far], out.at[far], p.core))
        yield
    for copy in cores:
        copy.wait_recv()
    keep.wait()


def gather8(w, p, own, out, half, local):
    c, cx = p.c, p.cx
    keep = pltpu.make_async_copy(own, out.at[c], local)
    keep.start()
    from_x = w.send(own, out.at[c], p.x_near)
    rings = [(w.send(own, out.at[c], p.z_up), w.send(own, out.at[c], p.z_dn), c)]
    yield
    from_x.wait_recv()
    rings.append((w.send(out.at[cx], out.at[cx], p.z_up), w.send(out.at[cx], out.at[cx], p.z_dn), cx))
    yield
    halves = []
    for up, down, slot in rings:
        up.wait_recv()
        part = out.at[lax.rem(slot + 6, 8), pl.ds(0, half)]
        halves.append(w.send(part, part, p.z_up))
        down.wait_recv()
        if half < own.shape[0]:
            part = out.at[lax.rem(slot + 2, 8), pl.ds(half, own.shape[0] - half)]
            halves.append(w.send(part, part, p.z_dn))
        yield
    for copy in halves:
        copy.wait_recv()
    keep.wait()


def ring_reduce(w, up, down, mine, far_up, far_down, near_up, near_down):
    a = w.send(mine(2, 0), far_up, up)
    b = w.send(mine(2, 1), far_down, down)
    yield
    c = w.send(mine(1, 1), near_up(1), up)
    d = w.send(mine(3, 0), near_down(0), down)
    yield
    a.wait_recv()
    far_up[...] = add_low(mine(1, 0)[...], far_up[...])
    e = w.send(far_up, near_up(0), up)
    b.wait_recv()
    far_down[...] = add_low(mine(3, 1)[...], far_down[...])
    g = w.send(far_down, near_down(1), down)
    yield
    for copy in (c, d, e, g):
        copy.wait_recv()


def reduce16(w, p, part, other, far, near, last, finish, produce=None):
    rows = other.shape[2]
    half = rows // 2
    order = (2, 1, 3, 0)
    arrivals = []
    for dy in order:
        for e in (0, 1):
            slot = lax.rem((p.f, p.fx)[e] + 4 * dy, 16)
            if produce is not None:
                produce(slot)
            arrivals.append(w.send(part(slot + 1 - 2 * p.k), other.at[dy, e], p.core))
    yield

    def merge(i, dy):
        for e in (0, 1):
            arrivals[2 * i + e].wait_recv()
            slot = lax.rem((p.f, p.fx)[e] + 4 * dy, 16)
            other[dy, e] = add_low(part(slot)[...], other[dy, e])

    spans = {0: pl.ds(0, half), 1: pl.ds(half, rows - half)}
    ring = ring_reduce(
        w,
        p.y_up,
        p.y_dn,
        lambda dy, h: other.at[dy, :, spans[h]],
        far.at[0],
        far.at[1],
        lambda h: near.at[0, :, spans[h]],
        lambda h: near.at[1, :, spans[h]],
    )
    merge(0, 2)
    next(ring)
    merge(1, 1)
    merge(2, 3)
    next(ring)
    merge(3, 0)
    yield
    next(ring)
    yield
    for _ in ring:
        pass
    other[0, 1] = (
        other[0, 1].astype(F32) + near[0, 1].astype(F32) + near[1, 1].astype(F32)
    ).astype(BF)
    copy = w.send(other.at[0, 1], last, p.x_far)
    yield
    total = other[0, 0].astype(F32) + near[0, 0].astype(F32) + near[1, 0].astype(F32)
    copy.wait_recv()
    finish(total + last[...].astype(F32))


def reduce16_scratch(rows, cols):
    return [
        pltpu.VMEM((4, 2, rows, cols), BF),
        pltpu.VMEM((2, 2, rows // 2, cols), BF),
        pltpu.VMEM((2, 2, rows, cols), BF),
        pltpu.VMEM((rows, cols), BF),
    ]


def remote_params(cid):
    return pltpu.CompilerParams(collective_id=cid, has_side_effects=True, vmem_limit_bytes=LIMIT)


def local_params():
    return pltpu.CompilerParams(vmem_limit_bytes=LIMIT)


def shaped(shape, dtype):
    return jax.ShapeDtypeStruct(shape, dtype)


def first_kernel(x, seg, wp, wo, g, cot, xs, segs, wps, wos, gs, cots, ssem, rsem, local):
    p = Place()
    w = Wire(ssem, rsem)
    greet([p.z_up, p.z_dn, p.x_near, p.y_up, p.y_dn, p.x_far, p.core])()
    run_all(
        [
            gather8(w, p, x, xs, 64, local.at[0]),
            gather8(w, p, seg, segs, 8, local.at[1]),
            gather16(w, p, wp, wps, 48, local.at[2]),
            gather16(w, p, wo, wos, 32, local.at[3]),
            gather16(w, p, g, gs, 16, local.at[4]),
            gather16(w, p, cot, cots, 64, local.at[5]),
        ]
    )
    w.done()


def first_gather(x, seg, wp, wo, g, cot):
    return pl.pallas_call(
        first_kernel,
        name="first_gather",
        out_shape=(
            shaped((8,) + x.shape, BF),
            shaped((8,) + seg.shape, jnp.int32),
            shaped((16,) + wp.shape, BF),
            shaped((16,) + wo.shape, BF),
            shaped((16,) + g.shape, F32),
            shaped((16,) + cot.shape, BF),
        ),
        in_specs=[ANY] * 6,
        out_specs=(ANY,) * 6,
        scratch_shapes=[
            pltpu.SemaphoreType.DMA((96,)),
            pltpu.SemaphoreType.DMA((96,)),
            pltpu.SemaphoreType.DMA((6,)),
        ],
        compiler_params=remote_params(1),
    )(x, seg, wp, wo, g, cot)


def lanes(shape):
    return lax.broadcasted_iota(jnp.int32, shape, len(shape) - 1)


def spin(v):
    first = lax.rem(lanes(v.shape), 64) < 32
    return jnp.where(first, pltpu.roll(v, 96, 1), pltpu.roll(v, 32, 1))


def head_sums(v):
    low = lanes(v.shape) < 64
    left = jnp.sum(jnp.where(low, v, 0.0), axis=-1, keepdims=True)
    right = jnp.sum(jnp.where(low, 0.0, v), axis=-1, keepdims=True)
    return jnp.where(low, left, right)


def split3(v):
    high = v.astype(BF).astype(F32)
    rest = v - high
    mid = rest.astype(BF).astype(F32)
    return high, mid, (rest - mid).astype(BF).astype(F32)


def columns3(v, base, shape):
    where = lanes(shape)
    high, mid, low = split3(v)
    return jnp.where(
        where == base, high, jnp.where(where == base + 1, mid, jnp.where(where == base + 2, low, 0.0))
    )


def attend_kernel(
    xs, segs, wps, gain, qk_gain, trig, normed, raw, qx, kx, vx, ctx_full, ctx_low, q_plain
):
    weights = wps[:, 0:64, :].reshape(1024, 256)
    place = lanes((8, 128))
    docs = lax.broadcasted_iota(jnp.int32, (8, 128), 0)
    spot = jnp.where(place == docs + 64, 1.0, 0.0)
    low = lanes((128, 128)) < 64

    def project(b, carry):
        x = xs[b].astype(F32)
        r = lax.rsqrt(jnp.mean(x * x, axis=-1, keepdims=True) + 1e-5)
        n = (x * r * gain[...]).astype(BF)
        normed[b] = n
        qkv = dot(n, weights)
        raw[b] = qkv
        q, kv = qkv[:, 0:128], qkv[:, 128:256]
        cos, sin = trig[0, b], trig[1, b]
        qn = q * lax.rsqrt(head_sums(q * q) * (1.0 / 64) + 1e-6) * qk_gain[0:1]
        q_rot = (qn * cos + spin(qn) * sin).astype(BF).astype(F32) * 0.125
        kn = kv * lax.rsqrt(head_sums(kv * kv) * (1.0 / 64) + 1e-6) * qk_gain[1:2]
        k_rot = kn * cos + spin(kn) * sin
        same = jnp.where(segs[b] == docs, 1.0, 0.0)
        doc = dot_tn(same, spot)
        bias = jnp.where((lanes((128, 128)) >= 64) & (lanes((128, 128)) < 72), (doc - 1.0) * NEG, 0.0)
        ones = jnp.where((lanes((128, 128)) >= 72) & (lanes((128, 128)) < 75), 1.0, 0.0)
        kx[b] = jnp.where(low, k_rot, doc + ones).astype(BF)
        one_v = jnp.where((lanes((128, 128)) >= 64) & (lanes((128, 128)) < 67), 1.0, 0.0)
        vx[b] = jnp.where(low, pltpu.roll(kv, 64, 1), one_v).astype(BF)
        q_plain[0, b] = jnp.where(low, q_rot, bias).astype(BF)
        q_plain[1, b] = jnp.where(low, pltpu.roll(q_rot, 64, 1), bias).astype(BF)
        return carry

    lax.fori_loop(0, 8, project, 0)
    k_all = kx[...].reshape(1024, 128)
    v_all = vx[...].reshape(1024, 128)

    def attend(b, carry):
        out = []
        for h in range(2):
            q = q_plain[h, b]
            e = jnp.exp(dot_nt(q, k_all)).astype(BF)
            o = dot(e, v_all)
            total = o[:, 64:65]
            out.append(o / total)
            keep = jnp.where(lanes((128, 128)) >= 72, 0.0, q.astype(F32))
            qx[h, b] = (keep + columns3(-jnp.log(total), 72, (128, 128))).astype(BF)
        both = jnp.where(low, out[0], pltpu.roll(out[1], 64, 1))
        ctx_full[b] = both
        ctx_low[b] = both.astype(BF)
        return carry

    lax.fori_loop(0, 8, attend, 0)


def attend(xs, segs, wps, gain, qk_gain, trig):
    return pl.pallas_call(
        attend_kernel,
        name="attend",
        out_shape=(
            shaped((8, 128, 1024), BF),
            shaped((8, 128, 256), F32),
            shaped((2, 8, 128, 128), BF),
            shaped((8, 128, 128), BF),
            shaped((8, 128, 128), BF),
            shaped((8, 128, 128), F32),
            shaped((8, 128, 128), BF),
        ),
        in_specs=[VM] * 6,
        out_specs=(VM,) * 7,
        scratch_shapes=[pltpu.VMEM((2, 8, 128, 128), BF)],
        compiler_params=local_params(),
    )(xs, segs, wps, gain, qk_gain, trig)


def middle_kernel(ctx, x, wos, gain, middle, ctx_rows, mids, rows, own, ssem, rsem, local):
    p = Place()
    w = Wire(ssem, rsem)
    greet([p.ctx_peer(i) for i in range(1, 8)] + [p.y_up, p.y_dn, p.x_far, p.core])()
    place = pl.ds(pl.multiple_of(p.c * 128, 128), 128)
    keep = pltpu.make_async_copy(ctx.at[p.c], rows.at[:, place], local.at[0])
    keep.start()
    arrivals = []
    for i in range(1, 8):
        to = lax.rem(p.c + i, 8)
        arrivals.append(w.send(ctx.at[to], rows.at[:, place], (to, p.f)))
    keep.wait()
    for copy in arrivals:
        copy.wait_recv()
    for t in range(4):
        cols = slice(256 * t, 256 * t + 256)
        middle[:, cols] = x[:, cols].astype(F32) + dot(rows[...], wos[:, cols])
    m = middle[...]
    r = lax.rsqrt(jnp.mean(m * m, axis=-1, keepdims=True) + 1e-5)
    own[...] = (m * r * gain[...]).astype(BF)
    ctx_rows[...] = rows[...]
    run_all([gather16(w, p, own, mids, 64, local.at[1])])
    w.done()


def middle_gather(ctx, x, wos, gain):
    return pl.pallas_call(
        middle_kernel,
        name="middle_gather",
        out_shape=(
            shaped((128, 1024), F32),
            shaped((128, 1024), BF),
            shaped((16, 128, 1024), BF),
        ),
        in_specs=[ANY, VM, VM, VM],
        out_specs=(VM, VM, ANY),
        scratch_shapes=[
            pltpu.VMEM((128, 1024), BF),
            pltpu.VMEM((128, 1024), BF),
            pltpu.SemaphoreType.DMA((32,)),
            pltpu.SemaphoreType.DMA((32,)),
            pltpu.SemaphoreType.DMA((2,)),
        ],
        compiler_params=remote_params(2),
    )(ctx, x, wos, gain)


LATE_IN = {
    "gs": VM,
    "mids": ANY,
    "cots": ANY,
    "wg": ANY,
    "wu": ANY,
    "wd": ANY,
    "middle": ((128, 1024), F32),
    "x": ((128, 1024), BF),
    "cot": ((128, 1024), BF),
    "wos": ANY,
    "ctx_rows": ((128, 1024), BF),
    "ctx_full": ((8, 128, 128), F32),
    "qx": ((2, 8, 128, 128), BF),
    "kx": ((8, 128, 128), BF),
    "vx": ((8, 128, 128), BF),
    "raw": ((8, 128, 256), F32),
    "normed": ANY,
    "xs": ANY,
    "wps": ((16, 80, 256), BF),
    "trig": ((2, 8, 128, 128), F32),
    "gain_in": VM,
    "gain_mid": VM,
    "qk_gain": VM,
}
LATE_OUT = {
    "output": ((128, 1024), BF, VM),
    "input_grad": ((128, 1024), F32, VM),
    "gu_all": ((2, 8, 128, 1024), BF, ANY),
    "d_all": ((2, 4, 128, 1024), BF, ANY),
    "w_all": ((8, 64, 256), BF, ANY),
    "out_all": ((8, 64, 128), BF, ANY),
    "small_sum": ((24, 128), F32, VM),
}
LATE_SCRATCH = {
    "table": ((32, 128), F32),
    "key": ((32, 128), F32),
    "hot": ((8, 2 * CAP * 2, 256), BF),
    "gate": ((8, 2, 2 * CAP, 128), F32),
    "mid_buf": ((16, 128, 1024), BF),
    "cot_buf": ((16, 128, 1024), BF),
    "wgu": ((2, 8, 128, 1024), BF),
    "wdb": ((8, 128, 1024), BF),
    "xin": ((8, 2, 2 * CAP, 1024), BF),
    "gout": ((8, 2, 2 * CAP, 1024), BF),
    "act": ((16 * CAP, 512), BF),
    "ggu": ((16 * CAP, 1024), BF),
    "dgu": ((2, 8, 128, 1024), BF),
    "ddn": ((2, 4, 128, 1024), BF),
    "ufar": ((2, 2, 128, 1024), BF),
    "unear": ((2, 2, 2, 128, 1024), BF),
    "ulast": ((2, 128, 1024), BF),
    "dx": ((4, 128, 1024), BF),
    "dfar": ((2, 64, 1024), BF),
    "dnear": ((2, 128, 1024), BF),
    "own_d": ((128, 1024), BF),
    "total": ((128, 1024), F32),
    "grad_middle": ((128, 1024), F32),
    "branch": ((128, 1024), BF),
    "back": ((128, 1024), BF),
    "dctx": ((8, 128, 128), BF),
    "gx": ((2, 8, 128, 128), BF),
    "dq": ((2, 1024, 128), F32),
    "dkv": ((8, 128, 128), BF),
    "dqkv": ((8, 128, 256), BF),
    "zfar": ((2, 2, 64, 1024), BF),
    "znear": ((2, 2, 128, 1024), BF),
    "zlast": ((128, 1024), BF),
    "zsend": ((128, 1024), BF),
    "w_own": ((64, 256), BF),
    "out_own": ((8, 64, 128), BF),
    "out_parts": ((7, 64, 128), BF),
    "out_mine": ((64, 128), BF),
    "small": ((24, 128), F32),
    "ctx_small": ((7, 24, 128), F32),
    "mid_small": ((24, 128), F32),
    "fsdp_small": ((16, 24, 128), F32),
}
COPIES = 224
FETCHES = 40


def ring_rows(slot, size):
    return pl.ds(pl.multiple_of(slot * size, size), size)


def late_kernel(*refs):
    names = list(LATE_IN) + list(LATE_OUT) + list(LATE_SCRATCH)
    r = SimpleNamespace(**dict(zip(names, refs)))
    rest = list(refs[len(names) :])
    staged = {n: rest.pop(0) for n, v in LATE_IN.items() if isinstance(v, tuple)}
    red_g, red_o, red_q, red_w = (rest[4 * i : 4 * i + 4] for i in range(4))
    ssem, rsem, lsem = rest[16:]
    p = Place()
    w = Wire(ssem, rsem)
    fetch = Fetch(lsem)
    arrived = greet(
        [p.ctx_peer(i) for i in range(1, 8)] + [p.fsdp_peer(i) for i in range(1, 16)]
    )
    fetch.go("cots", r.cots, r.cot_buf)
    fetch.go("mids", r.mids, r.mid_buf)
    for j in range(2):
        fetch.go("w", r.wg.at[j], r.wgu.at[j, :, :, pl.ds(0, 512)])
        fetch.go("w", r.wu.at[j], r.wgu.at[j, :, :, pl.ds(512, 512)])
    fetch.go("w", r.wd, r.wdb)
    for name, ref in staged.items():
        fetch.go(name, getattr(r, name), ref)
        setattr(r, name, ref)

    for s in range(16):
        r.table[2 * s : 2 * s + 2, :] = r.gs[s, pl.ds(2 * p.f, 2), :]
    named = r.table[...] > 0.0
    row = lax.broadcasted_iota(jnp.int32, (128, 128), 0)
    col = lax.broadcasted_iota(jnp.int32, (128, 128), 1)
    before = jnp.where(row < col, 1.0, 0.0).astype(BF)
    count = dot(jnp.where(named, 1.0, 0.0).astype(BF), before)
    odd = lax.rem(lax.broadcasted_iota(jnp.int32, (32, 128), 0) // 2, 2).astype(F32)
    r.key[...] = jnp.where(named, count + odd * CAP, -1.0)
    slot_id = lax.broadcasted_iota(jnp.int32, (2 * CAP, 256), 0).astype(F32)
    for q in range(8):
        for j in range(2):
            a, b = 4 * q + j, 4 * q + 2 + j
            keys = jnp.concatenate([r.key[a : a + 1, :], r.key[b : b + 1, :]], axis=1)
            vals = jnp.concatenate([r.table[a : a + 1, :], r.table[b : b + 1, :]], axis=1)
            chosen = slot_id == keys
            r.hot[q, 2 * CAP * j : 2 * CAP * (j + 1)] = jnp.where(chosen, 1.0, 0.0).astype(BF)
            weight = jnp.sum(jnp.where(chosen, vals, 0.0), axis=1, keepdims=True)
            r.gate[q, j] = jnp.broadcast_to(weight, (2 * CAP, 128))
    fetch.need("cots")
    for q in range(8):
        rows = dot(r.hot[q], r.cot_buf[2 * q : 2 * q + 2].reshape(256, 1024))
        weight = r.gate[q].reshape(4 * CAP, 128)[:, 0:1]
        r.gout[q] = (weight * rows).astype(BF).reshape(2, 2 * CAP, 1024)
    fetch.need("mids")
    for q in range(8):
        rows = dot(r.hot[q], r.mid_buf[2 * q : 2 * q + 2].reshape(256, 1024))
        r.xin[q] = rows.astype(BF).reshape(2, 2 * CAP, 1024)
    fetch.need("w")

    def expert(j):
        x = r.xin[:, j].reshape(16 * CAP, 1024)
        go = r.gout[:, j].reshape(16 * CAP, 1024)
        w_back = r.wdb[pl.ds(4 * j, 4)].reshape(512, 1024)
        for n in range(2):
            left, right = slice(256 * n, 256 * n + 256), slice(256 * n + 512, 256 * n + 768)
            gp = dot(x, r.wgu[j, :, :, left].reshape(1024, 256))
            up = dot(x, r.wgu[j, :, :, right].reshape(1024, 256))
            ga = dot_nt(go, w_back[left])
            s = 1.0 / (1.0 + jnp.exp(-gp))
            silu = gp * s
            r.act[:, left] = (silu * up).astype(BF)
            r.ggu[:, left] = (ga * up * (s * (1.0 + gp * (1.0 - s)))).astype(BF)
            r.ggu[:, right] = (ga * silu).astype(BF)
        for n in range(4):
            cols = slice(256 * n, 256 * n + 256)
            part = dot_tn(x[:, cols], r.ggu[...]).astype(BF)
            r.dgu[j, 2 * n : 2 * n + 2] = part.reshape(2, 128, 1024)
            r.ddn[j, :, :, cols] = dot_tn(r.act[...], go[:, cols]).astype(BF).reshape(4, 128, 256)
        weight = r.gate[:, j].reshape(16 * CAP, 128)[:, 0:1]
        for n in range(4):
            cols = slice(256 * n, 256 * n + 256)
            part = (weight * dot(r.act[...], w_back[:, cols])).astype(BF)
            r.xin[:, j, :, cols] = part.reshape(8, 2 * CAP, 256)
            part = dot_nt(r.ggu[...], r.wgu[j, 2 * n : 2 * n + 2].reshape(256, 1024))
            r.gout[:, j, :, cols] = part.astype(BF).reshape(8, 2 * CAP, 256)

    theirs, ours = 1 - p.xl, p.xl

    def ring_gu(i, e):
        def mine(d, h):
            return r.dgu.at[e, lax.rem(p.z + d, 4) * 2 + h]

        yield from ring_reduce(
            w,
            p.z_up,
            p.z_dn,
            mine,
            r.ufar.at[i, 0],
            r.ufar.at[i, 1],
            lambda h: r.unear.at[i, 0, h],
            lambda h: r.unear.at[i, 1, h],
        )

    def sum_gu(i, e):
        return (
            r.dgu[e, pl.ds(2 * p.z, 2)].astype(F32)
            + r.unear[i, 0].astype(F32)
            + r.unear[i, 1].astype(F32)
        )

    handed = {}

    def first_gu():
        yield from ring_gu(0, theirs)
        r.unear[0, 0] = sum_gu(0, theirs).astype(BF)
        handed["gu"] = w.send(r.unear.at[0, 0], r.ulast, p.x_near)

    def second_gu():
        yield from ring_gu(1, ours)
        total = sum_gu(1, ours)
        handed["gu"].wait_recv()
        r.ulast[...] = (total + r.ulast[...].astype(F32)).astype(BF)

        def slot(e, dz):
            return r.gu_all.at[e, pl.ds(lax.rem(p.z + dz, 4) * 2, 2)]

        def half(e, dz, h):
            return r.gu_all.at[e, lax.rem(p.z + dz, 4) * 2 + h]

        fetch.go("own_gu", r.ulast, slot(ours, 0))
        rings = [
            (
                w.send(r.ulast, slot(ours, 0), p.z_up),
                w.send(r.ulast, slot(ours, 0), p.z_dn),
                ours,
            )
        ]
        near = w.send(r.ulast, slot(ours, 0), p.x_near)
        yield
        near.wait_recv()
        rings.append(
            (
                w.send(slot(theirs, 0), slot(theirs, 0), p.z_up),
                w.send(slot(theirs, 0), slot(theirs, 0), p.z_dn),
                theirs,
            )
        )
        yield
        halves = []
        for up, down, e in rings:
            up.wait_recv()
            halves.append(w.send(half(e, 3, 0), half(e, 3, 0), p.z_up))
            down.wait_recv()
            halves.append(w.send(half(e, 1, 1), half(e, 1, 1), p.z_dn))
            yield
        for copy in halves:
            copy.wait_recv()
        fetch.need("own_gu")

    def downs():
        copy = w.send(r.ddn.at[theirs], r.dx, p.x_near)
        yield
        copy.wait_recv()
        r.dx[...] = add_low(r.ddn[ours], r.dx[...])
        spans = (pl.ds(0, 64), pl.ds(64, 64))
        ring = ring_reduce(
            w,
            p.z_up,
            p.z_dn,
            lambda d, h: r.dx.at[lax.rem(p.z + d, 4), spans[h]],
            r.dfar.at[0],
            r.dfar.at[1],
            lambda h: r.dnear.at[0, spans[h]],
            lambda h: r.dnear.at[1, spans[h]],
        )
        next(ring)
        yield from ring
        r.own_d[...] = (
            r.dx[p.z].astype(F32) + r.dnear[0].astype(F32) + r.dnear[1].astype(F32)
        ).astype(BF)

        def slot(dz):
            return r.d_all.at[ours, lax.rem(p.z + dz, 4)]

        def half(dz, h):
            return r.d_all.at[ours, lax.rem(p.z + dz, 4), spans[h]]

        fetch.go("own_d", r.own_d, slot(0))
        up = w.send(r.own_d, slot(0), p.z_up)
        down = w.send(r.own_d, slot(0), p.z_dn)
        near = [w.send(r.own_d, slot(0), p.x_near)]
        yield
        up.wait_recv()
        a = w.send(half(3, 0), half(3, 0), p.z_up)
        near.append(w.send(slot(3), slot(3), p.x_near))
        down.wait_recv()
        b = w.send(half(1, 1), half(1, 1), p.z_dn)
        near.append(w.send(slot(1), slot(1), p.x_near))
        yield
        a.wait_recv()
        b.wait_recv()
        near.append(w.send(slot(2), slot(2), p.x_near))
        yield
        for copy in near:
            copy.wait_recv()
        fetch.need("own_d")

    def combine(rows, out):
        def produce(slot):
            q = slot // 2
            both = dot_tn(r.hot[q], rows[q].reshape(4 * CAP, 1024))
            out[pl.ds(2 * q, 2)] = both.astype(BF).reshape(2, 128, 1024)

        return produce

    def keep_total(v):
        r.total[...] = v

    def write_output(v):
        r.output[...] = (r.middle[...] + v).astype(BF)

    gm = reduce16(w, p, lambda slot: r.cot_buf.at[slot], *red_g, keep_total, combine(r.gout, r.cot_buf))
    outs = reduce16(w, p, lambda slot: r.mid_buf.at[slot], *red_o, write_output, combine(r.xin, r.mid_buf))
    a, b, d = first_gu(), second_gu(), downs()

    arrived()
    expert(theirs)
    next(d)
    next(a)
    next(a)
    expert(ours)
    fetch.go("wos", r.wos, r.wgu.at[0])
    fetch.go("normed", r.normed, r.wgu.at[1])
    next(a)
    next(b)
    next(b)
    next(gm)
    next(d)
    fetch.need("middle")
    next(outs)
    next(gm)
    for _ in a:
        pass
    next(gm)
    next(outs)
    next(b)
    next(gm)
    next(d)
    for _ in gm:
        pass

    fetch.need("cot", "wos", "ctx_rows")
    m = r.middle[...]
    gy = r.total[...] * r.gain_mid[...]
    rm = lax.rsqrt(jnp.mean(m * m, axis=-1, keepdims=True) + 1e-5)
    inner = jnp.mean(gy * m, axis=-1, keepdims=True)
    gmid = r.cot[...].astype(F32) + rm * gy - m * (rm * rm * rm * inner)
    r.grad_middle[...] = gmid
    gain_sum = jnp.sum(r.total[...] * (m * rm), axis=0, keepdims=True)
    for i in range(8):
        r.small[8 + i : 9 + i, :] = gain_sum[:, 128 * i : 128 * i + 128]
    r.branch[...] = gmid.astype(BF)
    r.back[...] = dot_nt(r.branch[...], r.wgu[0].reshape(1024, 1024)).astype(BF)
    fetch.go("xs", r.xs, r.wgu.at[0])
    place = ring_rows(p.c, 128)
    fetch.go("dctx", r.back.at[:, place], r.dctx.at[p.c])
    arrivals = []
    for i in range(1, 8):
        to = lax.rem(p.c + i, 8)
        arrivals.append(w.send(r.back.at[:, ring_rows(to, 128)], r.dctx.at[p.c], (to, p.f)))
    next(outs)
    for n in range(4):
        part = dot_tn(r.ctx_rows[:, 256 * n : 256 * n + 256], r.branch[...]).astype(BF)
        r.xin[2 * n : 2 * n + 2, :, 0:64, :] = part.reshape(2, 2, 64, 1024)

    def grad_out(slot):
        return r.xin.at[slot // 2, lax.rem(slot, 2), pl.ds(0, 64)]

    def grad_w(slot):
        return r.gout.at[slot // 2, lax.rem(slot, 2), pl.ds(0, 64), pl.ds(0, 256)]


    def out_weight():
        def finish(v):
            for i in range(8):
                r.out_own[i] = v[:, 128 * i : 128 * i + 128].astype(BF)

        yield from reduce16(w, p, grad_out, *red_q, finish)
        arrivals = []
        for i in range(1, 8):
            to = lax.rem(p.c + i, 8)
            arrivals.append(w.send(r.out_own.at[to], r.out_parts.at[i - 1], (to, p.f)))
        yield
        sums = r.out_own[p.c].astype(F32)
        for i, copy in enumerate(arrivals):
            copy.wait_recv()
            sums = sums + r.out_parts[i].astype(F32)
        r.out_mine[...] = sums.astype(BF)
        yield
        yield from spread(r.out_mine, r.out_all, "out_mine")

    def spread(own, out, name):
        fetch.go(name, own, out.at[p.c])
        copies = [w.send(own, out.at[p.c], p.ctx_peer(i)) for i in range(1, 8)]
        yield
        for copy in copies:
            copy.wait_recv()
        fetch.need(name)

    ow = out_weight()
    next(ow)
    for copy in arrivals:
        copy.wait_recv()
    fetch.need("dctx", "ctx_full", "qx", "kx", "vx")

    low = lanes((128, 128)) < 64

    def prepare(b, carry):
        d = r.dctx[b].astype(F32)
        prod = d * r.ctx_full[b]
        left = jnp.sum(jnp.where(low, prod, 0.0), axis=-1, keepdims=True)
        right = jnp.sum(jnp.where(low, 0.0, prod), axis=-1, keepdims=True)
        r.gx[0, b] = jnp.where(low, d, columns3(-left, 64, (128, 128))).astype(BF)
        r.gx[1, b] = jnp.where(
            low, pltpu.roll(d, 64, 1), columns3(-right, 64, (128, 128))
        ).astype(BF)
        return carry

    lax.fori_loop(0, 8, prepare, 0)

    def block(i):
        at = slice(2 * i, 2 * i + 2)
        k = r.kx[at].reshape(256, 128)
        v = r.vx[at].reshape(256, 128)
        grad_k = jnp.zeros((256, 128), F32)
        grad_v = jnp.zeros((256, 128), F32)
        for h in range(2):
            q_all = r.qx[h].reshape(1024, 128)
            g_all = r.gx[h].reshape(1024, 128)
            pt = jnp.exp(dot_nt(k, q_all))
            dst = (pt * dot_nt(v, g_all)).astype(BF)
            grad_v = grad_v + dot(pt.astype(BF), g_all)
            grad_k = grad_k + dot(dst, q_all)
            part = dot_tn(dst, k)
            r.dq[h] = part if i == 0 else r.dq[h] + part
        both = jnp.where(lanes((256, 128)) < 64, grad_k, pltpu.roll(grad_v, 64, 1))
        r.dkv[at] = both.astype(BF).reshape(2, 128, 128)

    block(0)
    next(b)
    next(outs)
    block(1)
    next(ow)
    for _ in outs:
        pass
    block(2)
    next(d)
    next(ow)
    block(3)
    next(b)
    next(ow)
    fetch.need("raw", "wps", "trig", "xs", "normed", "x")

    weights = r.wps[:, 0:64, :].reshape(1024, 256)
    sums = [jnp.zeros((1, 1024), F32), jnp.zeros((1, 128), F32), jnp.zeros((1, 128), F32)]

    def finish(b):
        rows = ring_rows(b, 128)
        cos, sin = r.trig[0, b], r.trig[1, b]
        gq = jnp.where(low, r.dq[0, rows, :], pltpu.roll(r.dq[1, rows, :], 64, 1)) * 0.125
        gq = gq.astype(BF).astype(F32)
        gkv = r.dkv[b].astype(F32)
        gq = gq * cos - spin(gq) * sin
        gkv_rot = gkv * cos - spin(gkv) * sin
        q, kv = r.raw[b, :, 0:128], r.raw[b, :, 128:256]
        rq = lax.rsqrt(head_sums(q * q) * (1.0 / 64) + 1e-6)
        rk = lax.rsqrt(head_sums(kv * kv) * (1.0 / 64) + 1e-6)
        sums[1] = sums[1] + jnp.sum(gq * q * rq, axis=0, keepdims=True)
        sums[2] = sums[2] + jnp.sum(gkv_rot * kv * rk, axis=0, keepdims=True)
        gq = gq * r.qk_gain[0:1]
        gk = gkv_rot * r.qk_gain[1:2]
        gq = rq * gq - q * (rq * rq * rq) * (head_sums(gq * q) * (1.0 / 64))
        gk = rk * gk - kv * (rk * rk * rk) * (head_sums(gk * kv) * (1.0 / 64))
        gkv = jnp.where(low, gk, gkv)
        r.dqkv[b, :, 0:128] = gq.astype(BF)
        r.dqkv[b, :, 128:256] = gkv.astype(BF)
        gn = dot_nt(r.dqkv[b], weights)
        partial[b] = gn.astype(BF)
        x = r.wgu[0, b].astype(F32)
        rx = lax.rsqrt(jnp.mean(x * x, axis=-1, keepdims=True) + 1e-5)
        sums[0] = sums[0] + jnp.sum(gn * (x * rx), axis=0, keepdims=True)

    partial = r.wdb
    halves = (pl.ds(0, 64), pl.ds(64, 64))
    ring = ring_reduce(
        w,
        p.z_up,
        p.z_dn,
        lambda d, h: partial.at[pl.ds(lax.rem(p.z + d, 4) * 2, 2), halves[h]],
        r.zfar.at[0],
        r.zfar.at[1],
        lambda h: r.znear.at[0, :, halves[h]],
        lambda h: r.znear.at[1, :, halves[h]],
    )
    for dz in (2, 1, 3, 0):
        for e in (0, 1):
            finish(lax.rem(p.z + dz, 4) * 2 + e)
        if dz == 2:
            next(ring)
        if dz == 3:
            next(ring)

    def tokens():
        yield from ring

        def summed(e):
            return (
                partial[2 * p.z + e].astype(F32)
                + r.znear[0, e].astype(F32)
                + r.znear[1, e].astype(F32)
            )

        r.zsend[...] = summed(theirs).astype(BF)
        copy = w.send(r.zsend, r.zlast, p.x_near)
        yield
        total = summed(ours)
        copy.wait_recv()
        gy = (total + r.zlast[...].astype(F32)) * r.gain_in[...]
        v = r.x[...].astype(F32)
        rx = lax.rsqrt(jnp.mean(v * v, axis=-1, keepdims=True) + 1e-5)
        inner = jnp.mean(gy * v, axis=-1, keepdims=True)
        r.input_grad[...] = r.grad_middle[...] + rx * gy - v * (rx * rx * rx * inner)

    def projections():
        def keep(v):
            r.w_own[...] = v.astype(BF)

        yield from reduce16(w, p, grad_w, *red_w, keep)
        yield from spread(r.w_own, r.w_all, "w_own")

    def vectors():
        first = [w.send(r.small, r.ctx_small.at[i - 1], p.ctx_peer(i)) for i in range(1, 8)]
        yield
        total = r.small[...]
        for i, copy in enumerate(first):
            copy.wait_recv()
            total = total + r.ctx_small[i]
        r.mid_small[...] = total
        r.fsdp_small[p.f] = total
        second = [
            w.send(r.mid_small, r.fsdp_small.at[p.f], p.fsdp_peer(i)) for i in range(1, 16)
        ]
        yield
        for copy in second:
            copy.wait_recv()
        total = r.fsdp_small[0]
        for i in range(1, 16):
            total = total + r.fsdp_small[i]
        r.small_sum[...] = total

    norm_sum, q_sum, k_sum = sums
    for i in range(8):
        r.small[i : i + 1, :] = norm_sum[:, 128 * i : 128 * i + 128]
    q_sum = q_sum + pltpu.roll(q_sum, 64, 1)
    k_sum = jnp.where(lanes((1, 128)) < 64, q_sum, pltpu.roll(k_sum, 64, 1))
    r.small[16:24, :] = jnp.broadcast_to(k_sum, (8, 128))
    vec = vectors()
    next(vec)
    part = dot_tn(r.wgu[1].reshape(1024, 1024), r.dqkv[...].reshape(1024, 256))
    r.gout[:, :, 0:64, 0:256] = part.astype(BF).reshape(8, 2, 64, 256)
    pw = projections()
    next(pw)
    run_all([tokens(), pw, vec, ow, b, d])
    w.done()


def late(**given):
    staged = [v for v in LATE_IN.values() if isinstance(v, tuple)]
    in_specs = [ANY if isinstance(v, tuple) else v for v in LATE_IN.values()]
    return pl.pallas_call(
        late_kernel,
        name="late",
        out_shape=tuple(shaped(v[0], v[1]) for v in LATE_OUT.values()),
        in_specs=in_specs,
        out_specs=tuple(v[2] for v in LATE_OUT.values()),
        scratch_shapes=[pltpu.VMEM(*v) for v in LATE_SCRATCH.values()]
        + [pltpu.VMEM(*v) for v in staged]
        + reduce16_scratch(128, 1024)
        + reduce16_scratch(128, 1024)
        + reduce16_scratch(64, 1024)
        + reduce16_scratch(64, 256)
        + [
            pltpu.SemaphoreType.DMA((COPIES,)),
            pltpu.SemaphoreType.DMA((COPIES,)),
            pltpu.SemaphoreType.DMA((FETCHES,)),
        ],
        compiler_params=remote_params(3),
    )(*[given[n] for n in LATE_IN])


def trig_tables():
    index = np.arange(1024)
    stored = index // 64
    natural = np.where(stored % 2 == 0, stored // 2, 15 - stored // 2)
    pos = (natural * 64 + index % 64).astype(np.float32)
    freq = (10000.0 ** (-np.arange(32) * 2.0 / 64)).astype(np.float32)
    angle = (pos[:, None] * freq[None, :]).astype(np.float64)
    cos, sin = np.cos(angle), np.sin(angle)
    cos = np.concatenate([cos] * 4, axis=1)
    sin = np.concatenate([-sin, sin, -sin, sin], axis=1)
    return np.stack([cos, sin]).astype(np.float32).reshape(2, 8, 128, 128)


def on_device(
    inputs, segments, routes, gate_weights, cotangent, norm_in, norm_mid, q_gain, k_gain,
    w_query, w_key, w_value, w_out, w_gate, w_up, w_down,
):
    c = lax.axis_index("ctx")
    f = lax.axis_index("fsdp")
    x, cot = inputs[0], cotangent[0]
    trig = jnp.asarray(trig_tables())
    wp = jnp.concatenate(
        [
            lax.dynamic_slice(w_query, (0, 128 * c), (64, 128)),
            lax.dynamic_slice(w_key, (0, 64 * c), (64, 64)),
            lax.dynamic_slice(w_value, (0, 64 * c), (64, 64)),
        ],
        axis=1,
    )
    gains = jnp.pad(jnp.concatenate([norm_in, norm_mid])[None], ((0, 15), (0, 128)))
    wp = jnp.concatenate([wp, gains], axis=0)
    seg = jnp.broadcast_to(segments, (8, 128))
    expert_ids = jnp.arange(EXPERTS, dtype=jnp.int32)
    g = jnp.sum(
        jnp.where(
            routes[0].T[None, :, :] == expert_ids[:, None, None], gate_weights[0].T[None], 0.0
        ),
        axis=1,
    )
    ones = jnp.ones((64,), F32)
    qk_gain = jnp.stack(
        [
            jnp.concatenate([q_gain, q_gain]).astype(F32),
            jnp.concatenate([k_gain.astype(F32), ones]),
        ]
    )
    xs, segs, wps, wos, gs, cots = first_gather(x, seg, wp, w_out, g, cot)
    gain_in = wps[:, 64, 0:64].reshape(1, 1024).astype(F32)
    gain_mid = wps[:, 64, 64:128].reshape(1, 1024).astype(F32)
    wo_full = wos.reshape(1024, 1024)
    normed, raw, qx, kx, vx, ctx_full, ctx_low = attend(xs, segs, wps, gain_in, qk_gain, trig)
    middle, ctx_rows, mids = middle_gather(ctx_low, x, wo_full, gain_mid)
    output, input_grad, gu_all, d_all, w_all, out_all, small_sum = late(
        gs=gs,
        mids=mids,
        cots=cots,
        wg=w_gate.reshape(2, 8, 128, 512),
        wu=w_up.reshape(2, 8, 128, 512),
        wd=w_down.reshape(8, 128, 1024),
        middle=middle,
        x=x,
        cot=cot,
        wos=wos.reshape(8, 128, 1024),
        ctx_rows=ctx_rows,
        ctx_full=ctx_full,
        qx=qx,
        kx=kx,
        vx=vx,
        raw=raw,
        normed=normed,
        xs=xs,
        wps=wps,
        trig=trig,
        gain_in=gain_in,
        gain_mid=gain_mid,
        qk_gain=qk_gain,
    )
    gu = gu_all.reshape(2, 1024, 1024)
    grad_wq = w_all[:, :, 0:128].transpose(1, 0, 2).reshape(64, 1024).astype(F32)
    grad_wk = w_all[:, :, 128:192].transpose(1, 0, 2).reshape(64, 512).astype(F32)
    grad_wv = w_all[:, :, 192:256].transpose(1, 0, 2).reshape(64, 512).astype(F32)
    grad_wo = out_all.transpose(1, 0, 2).reshape(64, 1024).astype(F32)
    grad_norm_in = lax.dynamic_slice(small_sum[0:8].reshape(1024), (64 * f,), (64,))
    grad_norm_mid = lax.dynamic_slice(small_sum[8:16].reshape(1024), (64 * f,), (64,))
    return (
        output[None],
        input_grad[None],
        grad_norm_in,
        grad_norm_mid,
        small_sum[16, 0:64],
        small_sum[16, 64:128],
        grad_wq,
        grad_wk,
        grad_wv,
        grad_wo,
        gu[:, :, :512].astype(F32),
        gu[:, :, 512:].astype(F32),
        d_all.reshape(2, 512, 1024).astype(F32),
    )


def solution(mesh):
    rows = P("fsdp", "ctx", None)
    in_specs = (
        rows,
        P("fsdp", "ctx"),
        rows,
        rows,
        rows,
        P("fsdp"),
        P("fsdp"),
        P(),
        P(),
        P("fsdp", None),
        P("fsdp", None),
        P("fsdp", None),
        P("fsdp", None),
        P("fsdp", None, None),
        P("fsdp", None, None),
        P("fsdp", None, None),
    )
    out_specs = (
        rows,
        rows,
        P("fsdp"),
        P("fsdp"),
        P(),
        P(),
        P("fsdp", None),
        P("fsdp", None),
        P("fsdp", None),
        P("fsdp", None),
        P("fsdp", None, None),
        P("fsdp", None, None),
        P("fsdp", None, None),
    )
    return jax.shard_map(
        on_device, mesh=mesh, in_specs=in_specs, out_specs=out_specs, check_vma=False
    )
```
